512 devices in a mesh: leaf: 128 (over y, z, core), cols: 4 (over x).
Axes of the slice: x: 4, y: 8, z: 8, core: 2. Of those that a mesh axis runs over, the one named last changes fastest.
Arguments:
- samples: bfloat16 [262144, 256], P(('leaf', 'cols')), may hold values from -6 to 6
- near_tiles: bfloat16 [2048, 16, 128, 128], P('leaf', 'cols'), may hold values from -0.1875 to 0.1875
- columns: int32 [2048, 16], P('leaf', 'cols'), may hold values from 0 to 2047, as said below
- tile_count: int32 [2048], P('leaf'), may hold values from 4 to 16, as said below
- skeleton_one: int32 [16, 64, 128], P('cols'), may hold values from 0 to 255, as said below
- skeleton_two: int32 [16, 32, 128], P('cols'), may hold values from 0 to 255, as said below
- skeleton_three: int32 [16, 16, 128], P('cols'), may hold values from 0 to 255, as said below
Outputs:
- transfer_one: float32 [128, 8, 256, 128], P('leaf', 'cols')
- transfer_two: float32 [128, 4, 256, 128], P('leaf', 'cols')
- transfer_three: float32 [128, 4, 256, 128], P('leaf', 'cols')
- top_samples: float32 [128, 4, 128, 256], P('leaf', 'cols')
The draws below stay inside these ranges and needn't reach their ends.
Inputs may be any that keep to these rules, and one draw needn't show every extreme that they name: `columns`: the column cluster of a slot of row cluster r, of any layer, lies in region r // 16 or a region beside it. `tile_count`: slots at or past a cluster's count are unused; some cluster uses all 16. `skeleton_one`: each row holds 128 distinct indices. `skeleton_two`: each row holds 128 distinct indices. `skeleton_three`: each row holds 128 distinct indices.
All inputs are finite; a program needn't handle non-finite values.
Results may differ from the reference program's by a relative error of at most 0.0003.
Values may be sent and summed in bfloat16 or wider, within the bound.
No kernel may reach another device: no remote copies, remote signals or barrier semaphores. Data moves between devices by JAX's collectives and lax.ppermute only.
A program may use at most 64 MiB of HBM per device.

```python
import jax
import jax.numpy as jnp
from jax import lax

CL = 128
S = 256
KT = 16
KSUB = 4
LEVELS = 3
CLD = 16
NCL = 2048
NPAN = 262144
N_LEAF = 128
N_COLS = 4


def draw_columns(key, part):
    leaf_count = NCL // CLD
    owner = jnp.arange(NCL, dtype=jnp.int32) // CLD
    step = jax.random.randint(jax.random.fold_in(key, 1), (NCL, KT), -1, 2)
    device = jnp.clip(owner[:, None] + step, 0, leaf_count - 1)
    member = jax.random.randint(jax.random.fold_in(key, 2), (NCL, KT), 0, CLD)
    return (device * CLD + member).astype(jnp.int32)


def draw_tile_count(key, part):
    counts = jax.random.randint(jax.random.fold_in(key, 3), (NCL,), KT // 4, KT + 1)
    return counts.at[0].set(KT).astype(jnp.int32)


def draw_levels(key, groups, salt):
    keys = jax.random.split(jax.random.fold_in(key, salt), CLD * groups)
    perms = jax.vmap(lambda single: jax.random.permutation(single, 2 * CL))(keys)
    return perms[:, :CL].reshape(CLD, groups, CL).astype(jnp.int32)


def draw_skeleton_one(key, part):
    return draw_levels(key, NCL // CLD // 2, 11)


def draw_skeleton_two(key, part):
    return draw_levels(key, NCL // CLD // 4, 12)


def draw_skeleton_three(key, part):
    return draw_levels(key, NCL // CLD // 8, 13)


def level_of(own_key, extent, cuts, low, top_value):
    def one(dim, shards_of):
        draws = jax.random.uniform(jax.random.fold_in(jax.random.fold_in(own_key, 6), dim), (shards_of,), jnp.float32, low / len(cuts), top_value / len(cuts))
        return jnp.repeat(jnp.exp(draws), extent[dim] // shards_of).reshape((-1,) + (1,) * (len(extent) - dim - 1))

    factor_of = one(*cuts[0])
    for cut in cuts[1:]:
        factor_of = factor_of * one(*cut)
    return factor_of


def gaussian(own_key, shape, scale, limit, cuts=(), held_as=jnp.bfloat16):
    drawn = jax.random.normal(own_key, shape, jnp.float32) * scale
    if len(cuts) > 0:
        drawn = level_of(own_key, shape, cuts, -0.22, 0.18) * drawn
    return jnp.clip(drawn, min=-limit, max=limit).astype(held_as)


def setup_inputs(seed: int = 0) -> dict:
    streams_of = jax.random.split(jax.random.key(seed), 8)
    return {
        "samples": gaussian(streams_of[0], (NPAN, S), 1.0, 6.0, ((0, 512),)),
        "near_tiles": gaussian(streams_of[1], (NCL, KT, CL, CL), (CL * KT // 2) ** -0.5, 0.1875, ((0, 128), (1, 4))),
        "columns": draw_columns(jax.random.fold_in(streams_of[7], 71), 0),
        "tile_count": draw_tile_count(jax.random.fold_in(streams_of[7], 71), 0),
        "skeleton_one": draw_skeleton_one(jax.random.fold_in(streams_of[7], 71), 0),
        "skeleton_two": draw_skeleton_two(jax.random.fold_in(streams_of[7], 71), 0),
        "skeleton_three": draw_skeleton_three(jax.random.fold_in(streams_of[7], 71), 0),
    }


HIGHEST = lax.Precision.HIGHEST
RIDGE = 0.25

def merge_pair(first, second, chosen):
    stacked = jnp.concatenate([first, second], axis=1)
    picked = jax.vmap(lambda block, index: block[index])(stacked, chosen)
    count = stacked.shape[2]
    rank = picked.shape[1]
    gram = jnp.einsum('mis,mjs->mij', picked, picked, precision=HIGHEST) / count
    gram = gram + RIDGE * jnp.eye(rank, dtype=jnp.float32)
    lower = jnp.linalg.cholesky(gram)
    basis = jax.vmap(lambda factor, rhs: jax.scipy.linalg.solve_triangular(factor, rhs, lower=True))(lower, picked)
    transfer = jnp.einsum('mis,mjs->mij', stacked, basis, precision=HIGHEST) / count
    return (basis, transfer)

def arrange(full, level):
    spread = min(2 ** level, KSUB)
    per = KSUB // spread
    device = jnp.arange(N_LEAF, dtype=jnp.int32)
    group = device // 2 ** level
    column = jnp.arange(N_COLS * per, dtype=jnp.int32)
    member = (column // per)[None, :] * KSUB + (device % spread)[:, None] + spread * (column % per)[None, :]
    return full[group[:, None], member]

def reference(samples, near_tiles, columns, tile_count, skeleton_one, skeleton_two, skeleton_three):
    window = samples.reshape(NCL, CL, S)
    blocks = NCL // CLD

    def leaf_block(block):
        tiles_block, cols_block, count_block = block
        rows = window[cols_block].astype(jnp.float32)
        active = (jnp.arange(KT, dtype=jnp.int32)[None, :] < count_block[:, None]).astype(jnp.float32)
        rows = rows * active[:, :, None, None]
        return jnp.einsum('ksij,ksjn->kin', tiles_block.astype(jnp.float32), rows, precision=HIGHEST)
    nodes = lax.map(leaf_block, (near_tiles.reshape(blocks, CLD, KT, CL, CL), columns.reshape(blocks, CLD, KT), tile_count.reshape(blocks, CLD)))
    results = []
    level = 0
    for skeleton in (skeleton_one, skeleton_two, skeleton_three):
        level = level + 1
        first = nodes[0::2]
        second = nodes[1::2]
        chosen = jnp.swapaxes(skeleton, 0, 1)
        basis, transfer = lax.map(lambda block: merge_pair(block[0], block[1], block[2]), (first, second, chosen))
        results.append(arrange(transfer, level))
        nodes = basis
    top = arrange(nodes, LEVELS)
    return (results[0], results[1], results[2], top)
```

```python
import functools

import jax
import jax.numpy as jnp
from jax import lax
from jax.experimental import pallas as pl
from jax.experimental.pallas import tpu as pltpu
from jax.sharding import PartitionSpec as P

RIDGE = 0.25
BF = jnp.bfloat16
F32 = jnp.float32
PANEL = 16


def dot(a, b, ca, cb):
    return lax.dot_general(a, b, (((ca,), (cb,)), ((), ())), preferred_element_type=F32)


def split2(x):
    hi = x.astype(BF)
    lo = (x - hi.astype(F32)).astype(BF)
    return hi, lo


def split3(x):
    hi = x.astype(BF)
    rest = x - hi.astype(F32)
    mid = rest.astype(BF)
    lo = (rest - mid.astype(F32)).astype(BF)
    return hi, mid, lo


def near_kernel(
    info, cols, counts, own_tiles, tiles_a, tiles_b, tiles_c, before, own, after,
    send_ref, keep_ref, win, tiles, sem,
):
    x = info[0]
    even = info[1]
    late = info[2]
    copies = [
        pltpu.make_async_copy(own, win.at[pl.ds(2048, 2048)], sem.at[0]),
        pltpu.make_async_copy(before, win.at[pl.ds(0, 2048)], sem.at[1]),
        pltpu.make_async_copy(after, win.at[pl.ds(4096, 2048)], sem.at[2]),
        pltpu.make_async_copy(own_tiles.at[pl.ds(x * 4, 4)], tiles.at[0], sem.at[3]),
        pltpu.make_async_copy(tiles_a, tiles.at[1], sem.at[4]),
        pltpu.make_async_copy(tiles_b, tiles.at[2], sem.at[5]),
        pltpu.make_async_copy(tiles_c, tiles.at[3], sem.at[6]),
    ]
    for copy in copies:
        copy.start()
    for copy in copies:
        copy.wait()
    for q in range(4):
        keep, slot = divmod(q, 2)
        parity = even if keep == 1 else 1 - even
        member = late if slot == 1 else 1 - late
        k = parity + 2 * member
        count = counts[k]
        total = jnp.zeros((128, 256), F32)
        for delta in range(4):
            source = (x + 4 - delta) % 4
            for s in range(0, 4, 2):
                pieces = []
                rows = []
                for t in (s, s + 1):
                    place = source * 4 + t
                    live = jnp.where(place < count, 1.0, 0.0).astype(F32)
                    piece = tiles[delta, k, t]
                    pieces.append(piece * jnp.full((128, 128), live, F32).astype(BF))
                    col = jnp.clip(cols[k, place], 0, 47)
                    rows.append(win[pl.ds(pl.multiple_of(col * 128, 128), 128), :])
                total = total + dot(
                    jnp.concatenate(pieces, axis=1), jnp.concatenate(rows, axis=0), 1, 0
                )
        if keep == 1:
            keep_ref[slot] = total
        else:
            send_ref[slot] = total


def near(info, cols, counts, own_tiles, received, before, own, after):
    smem = pl.BlockSpec(memory_space=pltpu.SMEM)
    hbm = pl.BlockSpec(memory_space=pl.ANY)
    vmem = pl.BlockSpec(memory_space=pltpu.VMEM)
    block = jax.ShapeDtypeStruct((2, 128, 256), F32)
    return pl.pallas_call(
        near_kernel,
        out_shape=(block, block),
        in_specs=[smem] * 3 + [hbm] * 7,
        out_specs=(vmem, vmem),
        scratch_shapes=[
            pltpu.VMEM((6144, 256), BF),
            pltpu.VMEM((4, 4, 4, 128, 128), BF),
            pltpu.SemaphoreType.DMA((7,)),
        ],
        compiler_params=pltpu.CompilerParams(vmem_limit_bytes=24 << 20),
        cost_estimate=pl.CostEstimate(
            flops=540_000_000, bytes_accessed=6_000_000, transcendentals=0
        ),
    )(info, cols, counts, own_tiles, *received, before, own, after)


def eliminate(j, gram, rhs):
    base = j * PANEL
    half = PANEL // 2
    rows = lax.broadcasted_iota(jnp.int32, (half, 128), 0)
    a = [gram[base + half * h : base + half * (h + 1), :] for h in range(2)]
    body = [
        [a[h]] + [rhs[base + half * h : base + half * (h + 1), 128 * c : 128 * (c + 1)] for c in range(2)]
        for h in range(2)
    ]
    column = [
        [jnp.broadcast_to(a[h][:, base + k : base + k + 1], (half, 128)) for k in range(PANEL)]
        for h in range(2)
    ]
    scale = [jnp.zeros((half, 128), F32) for _ in range(2)]
    for i in range(PANEL):
        h0, r = divmod(i, half)
        pivot = column[h0][i][r : r + 1, :]
        inverse = lax.rsqrt(pivot)
        reciprocal = inverse * inverse
        scale[h0] = jnp.where(rows == r, jnp.broadcast_to(inverse, (half, 128)), scale[h0])
        factor = {}
        for h in range(h0, 2):
            value = column[h][i] * reciprocal
            factor[h] = jnp.where(rows > r, value, 0.0) if h == h0 else value
        for k in range(i + 1, PANEL):
            row = column[h0][k][r : r + 1, :]
            for h in range(h0, 2):
                column[h][k] = column[h][k] - factor[h] * row
        for c in range(3):
            row = body[h0][c][r : r + 1, :]
            for h in range(h0, 2):
                body[h][c] = body[h][c] - factor[h] * row
    return jnp.concatenate(
        [jnp.concatenate([body[h][c] * scale[h] for c in range(3)], axis=1) for h in range(2)],
        axis=0,
    )


def merge_kernel(nodes, own, other, choice, *refs):
    outs, gram = refs[:nodes], refs[nodes]
    for m in range(nodes):
        wide = [jnp.concatenate(pair, axis=0) for pair in zip(split3(own[m]), split3(other[m]))]
        hi, mid, lo = (dot(choice[m], part, 1, 0) for part in wide)
        outs[m][0] = hi + (mid + lo)
        hi = hi.astype(BF)
        mid = mid.astype(BF)
        product = dot(
            jnp.concatenate([hi, hi, mid], axis=1), jnp.concatenate([hi, mid, hi], axis=1), 1, 1
        )
        on = lax.broadcasted_iota(jnp.int32, (128, 128), 0) == lax.broadcasted_iota(
            jnp.int32, (128, 128), 1
        )
        gram[m] = product * (1.0 / 256) + jnp.where(on, RIDGE, 0.0)
    for j in range(128 // PANEL):
        done = (j + 1) * PANEL
        for m in range(nodes):
            rows = eliminate(j, gram.at[m], outs[m].at[0])
            outs[m][0, j * PANEL : done, :] = rows[:, 128:]
            if done < 128:
                hi, mid, lo = split3(rows)
                left = jnp.concatenate([hi, hi, mid, mid, hi, lo], axis=0)[:, :128]
                right = jnp.concatenate([hi, mid, hi, mid, lo, hi], axis=0)
                update = dot(left, right, 0, 0)
                gram[m, done:, :] = gram[m, done:, :] - update[done:, :128]
                outs[m][0, done:, :] = outs[m][0, done:, :] - update[done:, 128:]


def merge(own, other, choice):
    nodes = own.shape[0]
    vmem = pl.BlockSpec(memory_space=pltpu.VMEM)
    return pl.pallas_call(
        functools.partial(merge_kernel, nodes),
        out_shape=tuple(jax.ShapeDtypeStruct((1, 128, 256), F32) for _ in range(nodes)),
        in_specs=[vmem] * 3,
        out_specs=tuple(vmem for _ in range(nodes)),
        scratch_shapes=[pltpu.VMEM((nodes, 128, 128), F32)],
        compiler_params=pltpu.CompilerParams(vmem_limit_bytes=24 << 20),
        cost_estimate=pl.CostEstimate(
            flops=nodes * 40_000_000, bytes_accessed=nodes * 600_000, transcendentals=0
        ),
    )(own, other, choice)


def transfer_kernel(nodes, info, own, other, *refs):
    basis, out = refs[:nodes], refs[nodes]
    side = info[3]
    for m in range(nodes):
        place = 0 if nodes == 1 else (info[2] if m == 1 else 1 - info[2])
        zh, zl = split2(basis[m][0])
        right = jnp.concatenate([zh, zl, zh], axis=1)
        for part, at in ((own, side), (other, 1 - side)):
            ch, cl = split2(part[m])
            value = dot(jnp.concatenate([ch, ch, cl], axis=1), right, 1, 1) * (1.0 / 256)
            out[0, place, pl.ds(pl.multiple_of(at * 128, 128), 128), :] = value


def transfer(info, own, other, basis):
    nodes = len(basis)
    smem = pl.BlockSpec(memory_space=pltpu.SMEM)
    vmem = pl.BlockSpec(memory_space=pltpu.VMEM)
    return pl.pallas_call(
        functools.partial(transfer_kernel, nodes),
        out_shape=jax.ShapeDtypeStruct((1, nodes, 256, 128), F32),
        in_specs=[smem] + [vmem] * (2 + nodes),
        out_specs=vmem,
        compiler_params=pltpu.CompilerParams(vmem_limit_bytes=24 << 20),
        cost_estimate=pl.CostEstimate(
            flops=nodes * 50_000_000, bytes_accessed=nodes * 600_000, transcendentals=0
        ),
    )(info, own, other, *basis)


def shifted(value, axis, by):
    count = lax.axis_size(axis)
    return lax.ppermute(value, axis, [(i, (i + by) % count) for i in range(count)])


def swapped(value, apart):
    count = lax.axis_size("leaf")
    return lax.ppermute(value, "leaf", [(i, i ^ apart) for i in range(count)])


def one_hot(skeleton, group, members, side):
    chosen = lax.dynamic_slice_in_dim(skeleton, group, 1, axis=1)[:, 0]
    chosen = jnp.concatenate(
        [lax.dynamic_slice_in_dim(chosen, k, 1, axis=0) for k in members], axis=0
    )
    target = chosen + 128 * side - 256 * side * (chosen >= 128)
    return (target[:, :, None] == lax.broadcasted_iota(jnp.int32, (1, 1, 256), 2)).astype(BF)


def local(samples, near_tiles, columns, tile_count, skeleton_one, skeleton_two, skeleton_three):
    d = lax.axis_index("leaf")
    x = lax.axis_index("cols")
    b0, b1, b2 = d & 1, (d >> 1) & 1, (d >> 2) & 1
    infos = [jnp.stack([x, b0, b1, side]).astype(jnp.int32) for side in (b0, b1, b2)]

    own = lax.all_gather(samples, "cols", axis=0, tiled=True)
    received = [
        shifted(
            lax.dynamic_slice_in_dim(near_tiles, ((x + by) % 4) * 4, 4, axis=0), "cols", by
        )
        for by in (1, 2, 3)
    ]
    all_columns = lax.all_gather(columns - (d - 1) * 16, "cols", axis=0)
    cols = lax.dynamic_slice_in_dim(all_columns, x * 4, 4, axis=1)
    cols = jnp.swapaxes(cols, 0, 1).reshape(4, 16)
    counts = lax.dynamic_slice_in_dim(tile_count, x * 4, 4, axis=0)
    leaves = lax.axis_size("leaf")
    up = [(i, i + 1) for i in range(leaves - 1)]
    before = lax.ppermute(own, "leaf", up)
    after = lax.ppermute(own, "leaf", [(j, i) for i, j in up])

    choice_one = one_hot(skeleton_one, d >> 1, (b0 + 2 - 2 * b1, b0 + 2 * b1), b0)
    choice_two = one_hot(skeleton_two, d >> 2, (d & 3,), b1)
    choice_three = one_hot(skeleton_three, d >> 3, (d & 3,), b2)

    send, keep = near(infos[0], cols, counts, near_tiles, received, before, own, after)
    other = swapped(send, 1)
    away, basis = merge(keep, other, choice_one)
    arrived = swapped(away, 2)
    out_one = transfer(infos[0], keep, other, (away, basis))
    (basis_two,) = merge(basis, arrived, choice_two)
    arrived_two = swapped(basis_two, 4)
    out_two = transfer(infos[1], basis, arrived, (basis_two,))
    (top,) = merge(basis_two, arrived_two, choice_three)
    out_three = transfer(infos[2], basis_two, arrived_two, (top,))
    return out_one, out_two, out_three, top[None]


def solution(mesh):
    placed = (
        P(("leaf", "cols"), None),
        P("leaf", "cols", None, None),
        P("leaf", "cols"),
        P("leaf"),
        P("cols", None, None),
        P("cols", None, None),
        P("cols", None, None),
    )
    return jax.shard_map(
        local,
        mesh=mesh,
        in_specs=placed,
        out_specs=(P("leaf", "cols", None, None),) * 4,
        check_vma=False,
    )
```

```python
import functools

import jax
import jax.numpy as jnp
from jax import lax
from jax.experimental import pallas as pl
from jax.experimental.pallas import tpu as pltpu
from jax.sharding import PartitionSpec as P

RIDGE = 0.25
BF = jnp.bfloat16
F32 = jnp.float32
PANEL = 16


def dot(a, b, ca, cb):
    return lax.dot_general(a, b, (((ca,), (cb,)), ((), ())), preferred_element_type=F32)


def split2(x):
    hi = x.astype(BF)
    lo = (x - hi.astype(F32)).astype(BF)
    return hi, lo


def split3(x):
    hi = x.astype(BF)
    rest = x - hi.astype(F32)
    mid = rest.astype(BF)
    lo = (rest - mid.astype(F32)).astype(BF)
    return hi, mid, lo


def near_kernel(
    info, cols, counts, own_tiles, tiles_a, tiles_b, tiles_c, tiles_d, before, own, after,
    send_ref, keep_ref, win, tiles, sem,
):
    x = info[0]
    even = info[1]
    late = info[2]
    copies = [
        pltpu.make_async_copy(own, win.at[pl.ds(2048, 2048)], sem.at[0]),
        pltpu.make_async_copy(before, win.at[pl.ds(0, 2048)], sem.at[1]),
        pltpu.make_async_copy(after, win.at[pl.ds(4096, 2048)], sem.at[2]),
        pltpu.make_async_copy(own_tiles.at[pl.ds(x * 4, 4)], tiles.at[0], sem.at[3]),
        pltpu.make_async_copy(tiles_a.at[pl.ds(0, 4)], tiles.at[1], sem.at[4]),
        pltpu.make_async_copy(tiles_b, tiles.at[2, pl.ds(0, 2)], sem.at[5]),
        pltpu.make_async_copy(tiles_c, tiles.at[2, pl.ds(2, 2)], sem.at[6]),
        pltpu.make_async_copy(tiles_d.at[pl.ds(0, 4)], tiles.at[3], sem.at[7]),
    ]
    for copy in copies:
        copy.start()
    for copy in copies:
        copy.wait()
    for q in range(4):
        keep, slot = divmod(q, 2)
        parity = even if keep == 1 else 1 - even
        k = parity + 2 * (late if slot == 1 else 1 - late)
        count = counts[k]
        total = jnp.zeros((128, 256), F32)
        for delta in range(4):
            source = (x + 4 - delta) % 4
            for s in range(0, 4, 2):
                pieces = []
                rows = []
                for t in (s, s + 1):
                    place = source * 4 + t
                    live = jnp.where(place < count, 1.0, 0.0).astype(F32)
                    piece = tiles[delta, k, t]
                    pieces.append(piece * jnp.full((128, 128), live, F32).astype(BF))
                    col = jnp.clip(cols[delta * 4 + k, t], 0, 47)
                    member = col & 15
                    col = (col - member) + ((x - (member >> 2)) & 3) * 4 + (member & 3)
                    rows.append(win[pl.ds(pl.multiple_of(col * 128, 128), 128), :])
                total = total + dot(
                    jnp.concatenate(pieces, axis=1), jnp.concatenate(rows, axis=0), 1, 0
                )
        if keep == 1:
            keep_ref[slot] = total
        else:
            send_ref[slot] = total


def near(info, cols, counts, own_tiles, received, before, own, after):
    smem = pl.BlockSpec(memory_space=pltpu.SMEM)
    hbm = pl.BlockSpec(memory_space=pl.ANY)
    vmem = pl.BlockSpec(memory_space=pltpu.VMEM)
    block = jax.ShapeDtypeStruct((2, 128, 256), F32)
    return pl.pallas_call(
        near_kernel,
        out_shape=(block, block),
        in_specs=[smem] * 3 + [hbm] * 8,
        out_specs=(vmem, vmem),
        scratch_shapes=[
            pltpu.VMEM((6144, 256), BF),
            pltpu.VMEM((4, 4, 4, 128, 128), BF),
            pltpu.SemaphoreType.DMA((8,)),
        ],
        compiler_params=pltpu.CompilerParams(vmem_limit_bytes=24 << 20),
        cost_estimate=pl.CostEstimate(
            flops=540_000_000, bytes_accessed=6_000_000, transcendentals=0
        ),
    )(info, cols, counts, own_tiles, *received, before, own, after)


def eliminate(j, gram, rhs):
    base = j * PANEL
    half = PANEL // 2
    rows = lax.broadcasted_iota(jnp.int32, (half, 128), 0)
    a = [gram[base + half * h : base + half * (h + 1), :] for h in range(2)]
    body = [
        [a[h]] + [rhs[base + half * h : base + half * (h + 1), 128 * c : 128 * (c + 1)] for c in range(2)]
        for h in range(2)
    ]
    column = [
        [jnp.broadcast_to(a[h][:, base + k : base + k + 1], (half, 128)) for k in range(PANEL)]
        for h in range(2)
    ]
    scale = [jnp.zeros((half, 128), F32) for _ in range(2)]
    for i in range(PANEL):
        h0, r = divmod(i, half)
        pivot = column[h0][i][r : r + 1, :]
        inverse = lax.rsqrt(pivot)
        reciprocal = inverse * inverse
        scale[h0] = jnp.where(rows == r, jnp.broadcast_to(inverse, (half, 128)), scale[h0])
        factor = {}
        for h in range(h0, 2):
            value = column[h][i] * reciprocal
            factor[h] = jnp.where(rows > r, value, 0.0) if h == h0 else value
        for k in range(i + 1, PANEL):
            row = column[h0][k][r : r + 1, :]
            for h in range(h0, 2):
                column[h][k] = column[h][k] - factor[h] * row
        for c in range(3):
            row = body[h0][c][r : r + 1, :]
            for h in range(h0, 2):
                body[h][c] = body[h][c] - factor[h] * row
    return jnp.concatenate(
        [jnp.concatenate([body[h][c] * scale[h] for c in range(3)], axis=1) for h in range(2)],
        axis=0,
    )


def merge_kernel(nodes, own, other, choice, *refs):
    outs, gram = refs[:nodes], refs[nodes]
    for m in range(nodes):
        wide = [jnp.concatenate(pair, axis=0) for pair in zip(split3(own[m]), split3(other[m]))]
        hi, mid, lo = (dot(choice[m], part, 1, 0) for part in wide)
        outs[m][0] = hi + (mid + lo)
        hi = hi.astype(BF)
        mid = mid.astype(BF)
        product = dot(
            jnp.concatenate([hi, hi, mid], axis=1), jnp.concatenate([hi, mid, hi], axis=1), 1, 1
        )
        on = lax.broadcasted_iota(jnp.int32, (128, 128), 0) == lax.broadcasted_iota(
            jnp.int32, (128, 128), 1
        )
        gram[m] = product * (1.0 / 256) + jnp.where(on, RIDGE, 0.0)
    for j in range(128 // PANEL):
        done = (j + 1) * PANEL
        for m in range(nodes):
            rows = eliminate(j, gram.at[m], outs[m].at[0])
            outs[m][0, j * PANEL : done, :] = rows[:, 128:]
            if done < 128:
                hi, mid, lo = split3(rows)
                left = jnp.concatenate([hi, hi, mid, mid, hi, lo], axis=0)[:, :128]
                right = jnp.concatenate([hi, mid, hi, mid, lo, hi], axis=0)
                update = dot(left, right, 0, 0)
                gram[m, done:, :] = gram[m, done:, :] - update[done:, :128]
                outs[m][0, done:, :] = outs[m][0, done:, :] - update[done:, 128:]


def merge(own, other, choice):
    nodes = own.shape[0]
    vmem = pl.BlockSpec(memory_space=pltpu.VMEM)
    return pl.pallas_call(
        functools.partial(merge_kernel, nodes),
        out_shape=tuple(jax.ShapeDtypeStruct((1, 128, 256), F32) for _ in range(nodes)),
        in_specs=[vmem] * 3,
        out_specs=tuple(vmem for _ in range(nodes)),
        scratch_shapes=[pltpu.VMEM((nodes, 128, 128), F32)],
        compiler_params=pltpu.CompilerParams(vmem_limit_bytes=24 << 20),
        cost_estimate=pl.CostEstimate(
            flops=nodes * 40_000_000, bytes_accessed=nodes * 600_000, transcendentals=0
        ),
    )(own, other, choice)


def transfer_kernel(nodes, info, own, other, *refs):
    basis, out = refs[:nodes], refs[nodes]
    side = info[3]
    for m in range(nodes):
        place = 0 if nodes == 1 else (info[2] if m == 1 else 1 - info[2])
        zh, zl = split2(basis[m][0])
        right = jnp.concatenate([zh, zl, zh], axis=1)
        for part, at in ((own, side), (other, 1 - side)):
            ch, cl = split2(part[m])
            value = dot(jnp.concatenate([ch, ch, cl], axis=1), right, 1, 1) * (1.0 / 256)
            out[0, place, pl.ds(pl.multiple_of(at * 128, 128), 128), :] = value


def transfer(info, own, other, basis):
    nodes = len(basis)
    smem = pl.BlockSpec(memory_space=pltpu.SMEM)
    vmem = pl.BlockSpec(memory_space=pltpu.VMEM)
    return pl.pallas_call(
        functools.partial(transfer_kernel, nodes),
        out_shape=jax.ShapeDtypeStruct((1, nodes, 256, 128), F32),
        in_specs=[smem] + [vmem] * (2 + nodes),
        out_specs=vmem,
        compiler_params=pltpu.CompilerParams(vmem_limit_bytes=24 << 20),
        cost_estimate=pl.CostEstimate(
            flops=nodes * 50_000_000, bytes_accessed=nodes * 600_000, transcendentals=0
        ),
    )(info, own, other, *basis)


def shifted(value, axis, by):
    count = lax.axis_size(axis)
    return lax.ppermute(value, axis, [(i, (i + by) % count) for i in range(count)])


def swapped(value, apart):
    count = lax.axis_size("leaf")
    return lax.ppermute(value, "leaf", [(i, i ^ apart) for i in range(count)])


def one_hot(skeleton, group, members, side):
    chosen = lax.dynamic_slice_in_dim(skeleton, group, 1, axis=1)[:, 0]
    chosen = jnp.concatenate(
        [lax.dynamic_slice_in_dim(chosen, k, 1, axis=0) for k in members], axis=0
    )
    target = chosen + 128 * side - 256 * side * (chosen >= 128)
    return (target[:, :, None] == lax.broadcasted_iota(jnp.int32, (1, 1, 256), 2)).astype(BF)


def local(samples, near_tiles, columns, tile_count, skeleton_one, skeleton_two, skeleton_three):
    d = lax.axis_index("leaf")
    x = lax.axis_index("cols")
    b0, b1, b2 = d & 1, (d >> 1) & 1, (d >> 2) & 1
    infos = [jnp.stack([x, b0, b1, side]).astype(jnp.int32) for side in (b0, b1, b2)]

    near_columns = jnp.clip(columns - (d - 1) * 16, 0, 47).astype(BF)
    block = jnp.concatenate([samples, jnp.pad(near_columns, ((0, 0), (0, 252)))], axis=0)
    blocks = [block] + [shifted(block, "cols", by) for by in (1, 3, 2)]
    blocks = [blocks[0], blocks[1], blocks[3], blocks[2]]
    def tiles_of(by, start, size):
        return lax.dynamic_slice_in_dim(near_tiles, ((x + by) % 4) * 4 + start, size, axis=0)

    far_up = shifted(jnp.concatenate([tiles_of(1, 0, 4), tiles_of(2, 0, 2)]), "cols", 1)
    far_down = shifted(jnp.concatenate([tiles_of(3, 0, 4), tiles_of(2, 2, 2)]), "cols", 3)
    received = [
        far_up, shifted(far_up[4:], "cols", 1), shifted(far_down[4:], "cols", 3), far_down,
    ]
    own = jnp.concatenate([samples] + [part[:512] for part in blocks[1:]], axis=0)
    cols = jnp.stack([part[512:, :4] for part in blocks])
    cols = lax.dynamic_slice_in_dim(cols, x * 4, 4, axis=1).astype(jnp.int32).reshape(16, 4)
    counts = lax.dynamic_slice_in_dim(tile_count, x * 4, 4, axis=0)
    leaves = lax.axis_size("leaf")
    up = [(i, i + 1) for i in range(leaves - 1)]
    before = lax.ppermute(own, "leaf", up)
    after = lax.ppermute(own, "leaf", [(j, i) for i, j in up])

    choice_one = one_hot(skeleton_one, d >> 1, (b0 + 2 - 2 * b1, b0 + 2 * b1), b0)
    choice_two = one_hot(skeleton_two, d >> 2, (d & 3,), b1)
    choice_three = one_hot(skeleton_three, d >> 3, (d & 3,), b2)

    send, keep = near(infos[0], cols, counts, near_tiles, received, before, own, after)
    other = swapped(send, 1)
    away, basis = merge(keep, other, choice_one)
    arrived = swapped(away, 2)
    out_one = transfer(infos[0], keep, other, (away, basis))
    (basis_two,) = merge(basis, arrived, choice_two)
    arrived_two = swapped(basis_two, 4)
    out_two = transfer(infos[1], basis, arrived, (basis_two,))
    (top,) = merge(basis_two, arrived_two, choice_three)
    out_three = transfer(infos[2], basis_two, arrived_two, (top,))
    return out_one, out_two, out_three, top[None]


def solution(mesh):
    placed = (
        P(("leaf", "cols"), None),
        P("leaf", "cols", None, None),
        P("leaf", "cols"),
        P("leaf"),
        P("cols", None, None),
        P("cols", None, None),
        P("cols", None, None),
    )
    return jax.shard_map(
        local,
        mesh=mesh,
        in_specs=placed,
        out_specs=(P("leaf", "cols", None, None),) * 4,
        check_vma=False,
    )
```

```python
import functools

import jax
import jax.numpy as jnp
from jax import lax
from jax.experimental import pallas as pl
from jax.experimental.pallas import tpu as pltpu
from jax.sharding import PartitionSpec as P

RIDGE = 0.25
BF = jnp.bfloat16
F32 = jnp.float32
PANEL = 16


def dot(a, b, ca, cb):
    return lax.dot_general(a, b, (((ca,), (cb,)), ((), ())), preferred_element_type=F32)


def split2(x):
    hi = x.astype(BF)
    lo = (x - hi.astype(F32)).astype(BF)
    return hi, lo


def split3(x):
    hi = x.astype(BF)
    rest = x - hi.astype(F32)
    mid = rest.astype(BF)
    lo = (rest - mid.astype(F32)).astype(BF)
    return hi, mid, lo


ANY = pl.BlockSpec(memory_space=pl.ANY)
VMEM = pl.BlockSpec(memory_space=pltpu.VMEM)
SMEM = pl.BlockSpec(memory_space=pltpu.SMEM)
ROOM = pltpu.CompilerParams(vmem_limit_bytes=16 << 20)


def run(copies):
    for copy in copies:
        copy.start()
    for copy in copies:
        copy.wait()


def block_kernel(info, samples, columns, out, wide, extra, sem):
    body = pltpu.make_async_copy(samples, out.at[pl.ds(0, 512)], sem.at[0])
    body.start()
    wide[...] = jnp.zeros((16, 256), F32)
    wide[0:4, 0:16] = jnp.clip(columns[...] - info[4], 0, 47).astype(F32)
    extra[...] = wide[...].astype(BF)
    tail = pltpu.make_async_copy(extra, out.at[pl.ds(512, 16)], sem.at[1])
    tail.start()
    body.wait()
    tail.wait()


def sample_block(info, samples, columns):
    return pl.pallas_call(
        block_kernel,
        out_shape=jax.ShapeDtypeStruct((528, 256), BF),
        in_specs=[SMEM, ANY, VMEM],
        out_specs=ANY,
        scratch_shapes=[
            pltpu.VMEM((16, 256), F32),
            pltpu.VMEM((16, 256), BF),
            pltpu.SemaphoreType.DMA((2,)),
        ],
        compiler_params=ROOM,
    )(info, samples, columns.T)


def pack_kernel(info, tiles, up, down, sem):
    one, two, three = ((info[0] + by) % 4 * 4 for by in (1, 2, 3))
    run(
        [
            pltpu.make_async_copy(tiles.at[pl.ds(one, 4)], up.at[pl.ds(0, 4)], sem.at[0]),
            pltpu.make_async_copy(tiles.at[pl.ds(two, 2)], up.at[pl.ds(4, 2)], sem.at[1]),
            pltpu.make_async_copy(tiles.at[pl.ds(three, 4)], down.at[pl.ds(0, 4)], sem.at[2]),
            pltpu.make_async_copy(tiles.at[pl.ds(two + 2, 2)], down.at[pl.ds(4, 2)], sem.at[3]),
        ]
    )


def packed_tiles(info, tiles):
    block = jax.ShapeDtypeStruct((6, 4, 128, 128), BF)
    return pl.pallas_call(
        pack_kernel,
        out_shape=(block, block),
        in_specs=[SMEM, ANY],
        out_specs=(ANY, ANY),
        scratch_shapes=[pltpu.SemaphoreType.DMA((4,))],
        compiler_params=ROOM,
    )(info, tiles)


def forward_kernel(up, down, up_out, down_out, sem):
    run(
        [
            pltpu.make_async_copy(up.at[pl.ds(4, 2)], up_out, sem.at[0]),
            pltpu.make_async_copy(down.at[pl.ds(4, 2)], down_out, sem.at[1]),
        ]
    )


def forwarded(up, down):
    block = jax.ShapeDtypeStruct((2, 4, 128, 128), BF)
    return pl.pallas_call(
        forward_kernel,
        out_shape=(block, block),
        in_specs=[ANY, ANY],
        out_specs=(ANY, ANY),
        scratch_shapes=[pltpu.SemaphoreType.DMA((2,))],
        compiler_params=ROOM,
    )(up, down)


def gather_kernel(*refs):
    parts, own, columns, ids, sem = refs[:4], *refs[4:]
    copies = [
        pltpu.make_async_copy(part.at[pl.ds(0, 512)], own.at[pl.ds(512 * i, 512)], sem.at[i])
        for i, part in enumerate(parts)
    ]
    small = [
        pltpu.make_async_copy(part.at[pl.ds(512, 16)], ids.at[i], sem.at[4 + i])
        for i, part in enumerate(parts)
    ]
    for copy in copies + small:
        copy.start()
    for copy in small:
        copy.wait()
    for i in range(4):
        columns[16 * i : 16 * (i + 1), :] = ids[i][:, 0:128].astype(F32).astype(jnp.int32)
    for copy in copies:
        copy.wait()


def gathered(blocks):
    return pl.pallas_call(
        gather_kernel,
        out_shape=(
            jax.ShapeDtypeStruct((2048, 256), BF),
            jax.ShapeDtypeStruct((64, 128), jnp.int32),
        ),
        in_specs=[ANY] * 4,
        out_specs=(ANY, VMEM),
        scratch_shapes=[pltpu.VMEM((4, 16, 256), BF), pltpu.SemaphoreType.DMA((8,))],
        compiler_params=ROOM,
    )(*blocks)


def near_kernel(
    info, cols, counts, own_tiles, tiles_a, tiles_b, tiles_c, tiles_d, before, own, after,
    send_ref, keep_ref, win, tiles, sem,
):
    x = info[0]
    even = info[1]
    late = info[2]
    windows = [
        pltpu.make_async_copy(own, win.at[pl.ds(2048, 2048)], sem.at[0]),
        pltpu.make_async_copy(before, win.at[pl.ds(0, 2048)], sem.at[1]),
        pltpu.make_async_copy(after, win.at[pl.ds(4096, 2048)], sem.at[2]),
    ]
    arrivals = [
        [pltpu.make_async_copy(own_tiles.at[pl.ds(x * 4, 4)], tiles.at[0], sem.at[3])],
        [pltpu.make_async_copy(tiles_a.at[pl.ds(0, 4)], tiles.at[1], sem.at[4])],
        [
            pltpu.make_async_copy(tiles_b, tiles.at[2, pl.ds(0, 2)], sem.at[5]),
            pltpu.make_async_copy(tiles_c, tiles.at[2, pl.ds(2, 2)], sem.at[6]),
        ],
        [pltpu.make_async_copy(tiles_d.at[pl.ds(0, 4)], tiles.at[3], sem.at[7])],
    ]
    for copy in windows + sum(arrivals, []):
        copy.start()
    for copy in windows:
        copy.wait()
    for q in range(4):
        keep, slot = divmod(q, 2)
        parity = even if keep == 1 else 1 - even
        k = parity + 2 * (late if slot == 1 else 1 - late)
        count = counts[x * 4 + k]
        total = jnp.zeros((128, 256), F32)
        for delta in range(4):
            if q == 0:
                for copy in arrivals[delta]:
                    copy.wait()
            source = (x + 4 - delta) % 4
            for s in range(0, 4, 2):
                pieces = []
                rows = []
                for t in (s, s + 1):
                    place = source * 4 + t
                    live = jnp.where(place < count, 1.0, 0.0).astype(F32)
                    piece = tiles[delta, k, t]
                    pieces.append(piece * jnp.full((128, 128), live, F32).astype(BF))
                    col = jnp.clip(cols[delta * 16 + t, x * 4 + k], 0, 47)
                    member = col & 15
                    col = (col - member) + ((x - (member >> 2)) & 3) * 4 + (member & 3)
                    rows.append(win[pl.ds(pl.multiple_of(col * 128, 128), 128), :])
                total = total + dot(
                    jnp.concatenate(pieces, axis=1), jnp.concatenate(rows, axis=0), 1, 0
                )
        if keep == 1:
            keep_ref[slot] = total
        else:
            send_ref[slot] = total


def near(info, cols, counts, own_tiles, received, before, own, after):
    block = jax.ShapeDtypeStruct((2, 128, 256), F32)
    return pl.pallas_call(
        near_kernel,
        out_shape=(block, block),
        in_specs=[SMEM] * 3 + [ANY] * 8,
        out_specs=(VMEM, VMEM),
        scratch_shapes=[
            pltpu.VMEM((6144, 256), BF),
            pltpu.VMEM((4, 4, 4, 128, 128), BF),
            pltpu.SemaphoreType.DMA((8,)),
        ],
        compiler_params=ROOM,
        cost_estimate=pl.CostEstimate(
            flops=540_000_000, bytes_accessed=6_000_000, transcendentals=0
        ),
    )(info, cols, counts, own_tiles, *received, before, own, after)


def eliminate(j, gram, rhs):
    base = j * PANEL
    half = PANEL // 2
    rows = lax.broadcasted_iota(jnp.int32, (half, 128), 0)
    a = [gram[base + half * h : base + half * (h + 1), :] for h in range(2)]
    body = [
        [a[h]] + [rhs[base + half * h : base + half * (h + 1), 128 * c : 128 * (c + 1)] for c in range(2)]
        for h in range(2)
    ]
    column = [
        [jnp.broadcast_to(a[h][:, base + k : base + k + 1], (half, 128)) for k in range(PANEL)]
        for h in range(2)
    ]
    scale = [jnp.zeros((half, 128), F32) for _ in range(2)]
    for i in range(PANEL):
        h0, r = divmod(i, half)
        pivot = column[h0][i][r : r + 1, :]
        inverse = lax.rsqrt(pivot)
        reciprocal = inverse * inverse
        scale[h0] = jnp.where(rows == r, jnp.broadcast_to(inverse, (half, 128)), scale[h0])
        factor = {}
        for h in range(h0, 2):
            value = column[h][i] * reciprocal
            factor[h] = jnp.where(rows > r, value, 0.0) if h == h0 else value
        for k in range(i + 1, PANEL):
            row = column[h0][k][r : r + 1, :]
            for h in range(h0, 2):
                column[h][k] = column[h][k] - factor[h] * row
        for c in range(3):
            row = body[h0][c][r : r + 1, :]
            for h in range(h0, 2):
                body[h][c] = body[h][c] - factor[h] * row
    return jnp.concatenate(
        [jnp.concatenate([body[h][c] * scale[h] for c in range(3)], axis=1) for h in range(2)],
        axis=0,
    )


def put_transfer(out, place, side, own, other, basis):
    zh, zl = split2(basis)
    right = jnp.concatenate([zh, zl, zh], axis=1)
    for part, at in ((own, side), (other, 1 - side)):
        ch, cl = split2(part)
        value = dot(jnp.concatenate([ch, ch, cl], axis=1), right, 1, 1) * (1.0 / 256)
        out[0, place, pl.ds(pl.multiple_of(at * 128, 128), 128), :] = value


def merge_kernel(m, last, info, own, other, choice, out, *refs):
    gram = refs[-1]
    wide = [jnp.concatenate(pair, axis=0) for pair in zip(split3(own[m]), split3(other[m]))]
    hi, mid, lo = (dot(choice[m], part, 1, 0) for part in wide)
    out[0] = hi + (mid + lo)
    hi = hi.astype(BF)
    mid = mid.astype(BF)
    product = dot(
        jnp.concatenate([hi, hi, mid], axis=1), jnp.concatenate([hi, mid, hi], axis=1), 1, 1
    )
    on = lax.broadcasted_iota(jnp.int32, (128, 128), 0) == lax.broadcasted_iota(
        jnp.int32, (128, 128), 1
    )
    gram[...] = product * (1.0 / 256) + jnp.where(on, RIDGE, 0.0)
    for j in range(128 // PANEL):
        done = (j + 1) * PANEL
        rows = eliminate(j, gram, out.at[0])
        out[0, j * PANEL : done, :] = rows[:, 128:]
        if done < 128:
            hi, mid, lo = split3(rows)
            left = jnp.concatenate([hi, hi, mid, mid, hi, lo], axis=0)[:, :128]
            right = jnp.concatenate([hi, mid, hi, mid, lo, hi], axis=0)
            update = dot(left, right, 0, 0)
            gram[done:, :] = gram[done:, :] - update[done:, :128]
            out[0, done:, :] = out[0, done:, :] - update[done:, 128:]
    if last:
        put_transfer(refs[0], 0, info[3], own[m], other[m], out[0])


def merge(info, own, other, choice, m=0, last=False):
    shapes = [jax.ShapeDtypeStruct((1, 128, 256), F32)]
    if last:
        shapes.append(jax.ShapeDtypeStruct((1, 1, 256, 128), F32))
    return pl.pallas_call(
        functools.partial(merge_kernel, m, last),
        out_shape=tuple(shapes),
        in_specs=[SMEM] + [VMEM] * 3,
        out_specs=(VMEM,) * len(shapes),
        scratch_shapes=[pltpu.VMEM((128, 128), F32)],
        compiler_params=pltpu.CompilerParams(vmem_limit_bytes=24 << 20),
        cost_estimate=pl.CostEstimate(
            flops=4_000_000_000, bytes_accessed=600_000, transcendentals=0
        ),
    )(info, own, other, choice)


def transfer_kernel(nodes, info, own, other, *refs):
    basis, out = refs[:nodes], refs[nodes]
    for m in range(nodes):
        place = 0 if nodes == 1 else (info[2] if m == 1 else 1 - info[2])
        put_transfer(out, place, info[3], own[m], other[m], basis[m][0])


def transfer(info, own, other, basis):
    nodes = len(basis)
    return pl.pallas_call(
        functools.partial(transfer_kernel, nodes),
        out_shape=jax.ShapeDtypeStruct((1, nodes, 256, 128), F32),
        in_specs=[SMEM] + [VMEM] * (2 + nodes),
        out_specs=VMEM,
        compiler_params=pltpu.CompilerParams(vmem_limit_bytes=24 << 20),
        cost_estimate=pl.CostEstimate(
            flops=nodes * 50_000_000, bytes_accessed=nodes * 600_000, transcendentals=0
        ),
    )(info, own, other, *basis)


def shifted(value, axis, by):
    count = lax.axis_size(axis)
    return lax.ppermute(value, axis, [(i, (i + by) % count) for i in range(count)])


def swapped(value, apart):
    count = lax.axis_size("leaf")
    return lax.ppermute(value, "leaf", [(i, i ^ apart) for i in range(count)])


def one_hot(skeleton, group, members, side):
    chosen = lax.dynamic_slice_in_dim(skeleton, group, 1, axis=1)[:, 0]
    chosen = jnp.concatenate(
        [lax.dynamic_slice_in_dim(chosen, k, 1, axis=0) for k in members], axis=0
    )
    target = chosen + 128 * side - 256 * side * (chosen >= 128)
    return (target[:, :, None] == lax.broadcasted_iota(jnp.int32, (1, 1, 256), 2)).astype(BF)


def local(samples, near_tiles, columns, tile_count, skeleton_one, skeleton_two, skeleton_three):
    d = lax.axis_index("leaf")
    x = lax.axis_index("cols")
    b0, b1, b2 = d & 1, (d >> 1) & 1, (d >> 2) & 1
    infos = [
        jnp.stack([x, b0, b1, side, (d - 1) * 16]).astype(jnp.int32) for side in (b0, b1, b2)
    ]

    block = sample_block(infos[0], samples, columns)
    by_one, by_three, by_two = (shifted(block, "cols", by) for by in (1, 3, 2))
    up, down = packed_tiles(infos[0], near_tiles)
    far_up = shifted(up, "cols", 1)
    far_down = shifted(down, "cols", 3)
    next_up, next_down = forwarded(far_up, far_down)
    received = [far_up, shifted(next_up, "cols", 1), shifted(next_down, "cols", 3), far_down]
    own, cols = gathered([block, by_one, by_two, by_three])
    leaves = lax.axis_size("leaf")
    rising = [(i, i + 1) for i in range(leaves - 1)]
    before = lax.ppermute(own, "leaf", rising)
    after = lax.ppermute(own, "leaf", [(j, i) for i, j in rising])

    choice_one = one_hot(skeleton_one, d >> 1, (b0 + 2 - 2 * b1, b0 + 2 * b1), b0)
    choice_two = one_hot(skeleton_two, d >> 2, (d & 3,), b1)
    choice_three = one_hot(skeleton_three, d >> 3, (d & 3,), b2)

    send, keep = near(
        infos[0], cols, tile_count, near_tiles, received, before, own, after
    )
    other = swapped(send, 1)
    (away,) = merge(infos[0], keep, other, choice_one, 0)
    arrived = swapped(away, 2)
    (basis,) = merge(infos[0], keep, other, choice_one, 1)
    out_one = transfer(infos[0], keep, other, (away, basis))
    (basis_two,) = merge(infos[1], basis, arrived, choice_two)
    arrived_two = swapped(basis_two, 4)
    out_two = transfer(infos[1], basis, arrived, (basis_two,))
    top, out_three = merge(infos[2], basis_two, arrived_two, choice_three, last=True)
    return out_one, out_two, out_three, top[None]


def solution(mesh):
    placed = (
        P(("leaf", "cols"), None),
        P("leaf", "cols", None, None),
        P("leaf", "cols"),
        P("leaf"),
        P("cols", None, None),
        P("cols", None, None),
        P("cols", None, None),
    )
    return jax.shard_map(
        local,
        mesh=mesh,
        in_specs=placed,
        out_specs=(P("leaf", "cols", None, None),) * 4,
        check_vma=False,
    )
```

```python
import functools

import jax
import jax.numpy as jnp
from jax import lax
from jax.experimental import pallas as pl
from jax.experimental.pallas import tpu as pltpu
from jax.sharding import PartitionSpec as P

RIDGE = 0.25
BF = jnp.bfloat16
F32 = jnp.float32
PANEL = 16


def dot(a, b, ca, cb):
    return lax.dot_general(a, b, (((ca,), (cb,)), ((), ())), preferred_element_type=F32)


def split2(x):
    hi = x.astype(BF)
    lo = (x - hi.astype(F32)).astype(BF)
    return hi, lo


def split3(x):
    hi = x.astype(BF)
    rest = x - hi.astype(F32)
    mid = rest.astype(BF)
    lo = (rest - mid.astype(F32)).astype(BF)
    return hi, mid, lo


ANY = pl.BlockSpec(memory_space=pl.ANY)
VMEM = pl.BlockSpec(memory_space=pltpu.VMEM)
SMEM = pl.BlockSpec(memory_space=pltpu.SMEM)
ROOM = pltpu.CompilerParams(vmem_limit_bytes=16 << 20)


def gather_kernel(*refs):
    parts, own, columns, ids, sem = refs[:4], *refs[4:]
    copies = [
        pltpu.make_async_copy(part.at[pl.ds(0, 512)], own.at[pl.ds(512 * i, 512)], sem.at[i])
        for i, part in enumerate(parts)
    ]
    small = [
        pltpu.make_async_copy(part.at[pl.ds(512, 16)], ids.at[i], sem.at[4 + i])
        for i, part in enumerate(parts)
    ]
    for copy in copies + small:
        copy.start()
    for copy in small:
        copy.wait()
    for i in range(4):
        columns[4 * i : 4 * (i + 1), :] = ids[i].astype(F32)[0:4, 0:128].astype(jnp.int32)
    for copy in copies:
        copy.wait()


def gathered(blocks):
    return pl.pallas_call(
        gather_kernel,
        out_shape=(
            jax.ShapeDtypeStruct((2048, 256), BF),
            jax.ShapeDtypeStruct((16, 128), jnp.int32),
        ),
        in_specs=[ANY] * 4,
        out_specs=(ANY, VMEM),
        scratch_shapes=[pltpu.VMEM((4, 16, 256), BF), pltpu.SemaphoreType.DMA((8,))],
        compiler_params=pltpu.CompilerParams(vmem_limit_bytes=4 << 20),
    )(*blocks)


def near_kernel(
    info, cols, counts, own_tiles, tiles_a, tiles_b, tiles_c, before, own, after,
    send_ref, keep_ref, win, tiles, sem,
):
    x = info[0]
    even = info[1]
    late = info[2]
    windows = [
        pltpu.make_async_copy(own, win.at[pl.ds(2048, 2048)], sem.at[0]),
        pltpu.make_async_copy(before, win.at[pl.ds(0, 2048)], sem.at[1]),
        pltpu.make_async_copy(after, win.at[pl.ds(4096, 2048)], sem.at[2]),
    ]
    arrivals = [pltpu.make_async_copy(own_tiles.at[pl.ds(x * 4, 4)], tiles.at[0], sem.at[3])]
    arrivals += [
        pltpu.make_async_copy(part, tiles.at[i + 1], sem.at[i + 4])
        for i, part in enumerate((tiles_a, tiles_b, tiles_c))
    ]
    for copy in windows + arrivals:
        copy.start()
    for copy in windows:
        copy.wait()
    for q in range(4):
        keep, slot = divmod(q, 2)
        parity = even if keep == 1 else 1 - even
        k = parity + 2 * (late if slot == 1 else 1 - late)
        count = counts[x * 4 + k]
        total = jnp.zeros((128, 256), F32)
        for delta in range(4):
            if q == 0:
                arrivals[delta].wait()
            source = (x + 4 - delta) % 4
            for s in range(0, 4, 2):
                pieces = []
                rows = []
                for t in (s, s + 1):
                    place = source * 4 + t
                    live = jnp.where(place < count, 1.0, 0.0).astype(F32)
                    piece = tiles[delta, k, t]
                    pieces.append(piece * jnp.full((128, 128), live, F32).astype(BF))
                    col = jnp.clip(cols[delta * 4 + t, x * 4 + k], 0, 47)
                    member = col & 15
                    col = (col - member) + ((x - (member >> 2)) & 3) * 4 + (member & 3)
                    rows.append(win[pl.ds(pl.multiple_of(col * 128, 128), 128), :])
                total = total + dot(
                    jnp.concatenate(pieces, axis=1), jnp.concatenate(rows, axis=0), 1, 0
                )
        if keep == 1:
            keep_ref[slot] = total
        else:
            send_ref[slot] = total


def near(info, cols, counts, own_tiles, received, before, own, after):
    block = jax.ShapeDtypeStruct((2, 128, 256), F32)
    return pl.pallas_call(
        near_kernel,
        out_shape=(block, block),
        in_specs=[SMEM] * 3 + [ANY] * 7,
        out_specs=(VMEM, VMEM),
        scratch_shapes=[
            pltpu.VMEM((6144, 256), BF),
            pltpu.VMEM((4, 4, 4, 128, 128), BF),
            pltpu.SemaphoreType.DMA((7,)),
        ],
        compiler_params=ROOM,
        cost_estimate=pl.CostEstimate(
            flops=540_000_000, bytes_accessed=6_000_000, transcendentals=0
        ),
    )(info, cols, counts, own_tiles, *received, before, own, after)


def eliminate(j, gram, rhs):
    base = j * PANEL
    half = PANEL // 2
    rows = lax.broadcasted_iota(jnp.int32, (half, 128), 0)
    a = [gram[base + half * h : base + half * (h + 1), :] for h in range(2)]
    body = [
        [a[h]] + [rhs[base + half * h : base + half * (h + 1), 128 * c : 128 * (c + 1)] for c in range(2)]
        for h in range(2)
    ]
    column = [
        [jnp.broadcast_to(a[h][:, base + k : base + k + 1], (half, 128)) for k in range(PANEL)]
        for h in range(2)
    ]
    scale = [jnp.zeros((half, 128), F32) for _ in range(2)]
    for i in range(PANEL):
        h0, r = divmod(i, half)
        pivot = column[h0][i][r : r + 1, :]
        inverse = lax.rsqrt(pivot)
        reciprocal = inverse * inverse
        scale[h0] = jnp.where(rows == r, jnp.broadcast_to(inverse, (half, 128)), scale[h0])
        factor = {}
        for h in range(h0, 2):
            value = column[h][i] * reciprocal
            factor[h] = jnp.where(rows > r, value, 0.0) if h == h0 else value
        for k in range(i + 1, PANEL):
            row = column[h0][k][r : r + 1, :]
            for h in range(h0, 2):
                column[h][k] = column[h][k] - factor[h] * row
        for c in range(3):
            row = body[h0][c][r : r + 1, :]
            for h in range(h0, 2):
                body[h][c] = body[h][c] - factor[h] * row
    return jnp.concatenate(
        [jnp.concatenate([body[h][c] * scale[h] for c in range(3)], axis=1) for h in range(2)],
        axis=0,
    )


def put_transfer(out, place, side, own, other, basis):
    zh, zl = split2(basis)
    right = jnp.concatenate([zh, zl, zh], axis=1)
    for part, at in ((own, side), (other, 1 - side)):
        ch, cl = split2(part)
        value = dot(jnp.concatenate([ch, ch, cl], axis=1), right, 1, 1) * (1.0 / 256)
        out[0, place, pl.ds(pl.multiple_of(at * 128, 128), 128), :] = value


def merge_kernel(nodes, last, *refs):
    info = None
    if last:
        info, refs = refs[0], refs[1:]
    own, other, choice = refs[:3]
    outs, gram = refs[3 : 3 + nodes], refs[-1]
    for m in range(nodes):
        wide = [jnp.concatenate(pair, axis=0) for pair in zip(split3(own[m]), split3(other[m]))]
        hi, mid, lo = (dot(choice[m], part, 1, 0) for part in wide)
        outs[m][0] = hi + (mid + lo)
        hi = hi.astype(BF)
        mid = mid.astype(BF)
        product = dot(
            jnp.concatenate([hi, hi, mid], axis=1), jnp.concatenate([hi, mid, hi], axis=1), 1, 1
        )
        on = lax.broadcasted_iota(jnp.int32, (128, 128), 0) == lax.broadcasted_iota(
            jnp.int32, (128, 128), 1
        )
        gram[m] = product * (1.0 / 256) + jnp.where(on, RIDGE, 0.0)
    for j in range(128 // PANEL):
        done = (j + 1) * PANEL
        for m in range(nodes):
            rows = eliminate(j, gram.at[m], outs[m].at[0])
            outs[m][0, j * PANEL : done, :] = rows[:, 128:]
            if done < 128:
                hi, mid, lo = split3(rows)
                left = jnp.concatenate([hi, hi, mid, mid, hi, lo], axis=0)[:, :128]
                right = jnp.concatenate([hi, mid, hi, mid, lo, hi], axis=0)
                update = dot(left, right, 0, 0)
                gram[m, done:, :] = gram[m, done:, :] - update[done:, :128]
                outs[m][0, done:, :] = outs[m][0, done:, :] - update[done:, 128:]
    if last:
        put_transfer(refs[3 + nodes], 0, info[3], own[0], other[0], outs[0][0])


def merge(own, other, choice, info=None):
    nodes = own.shape[0]
    last = info is not None
    shapes = [jax.ShapeDtypeStruct((1, 128, 256), F32)] * nodes
    if last:
        shapes.append(jax.ShapeDtypeStruct((1, 1, 256, 128), F32))
    return pl.pallas_call(
        functools.partial(merge_kernel, nodes, last),
        out_shape=tuple(shapes),
        in_specs=[SMEM] * last + [VMEM] * 3,
        out_specs=(VMEM,) * len(shapes),
        scratch_shapes=[pltpu.VMEM((nodes, 128, 128), F32)],
        compiler_params=ROOM,
        cost_estimate=pl.CostEstimate(
            flops=nodes * 40_000_000, bytes_accessed=nodes * 600_000, transcendentals=0
        ),
    )(*([info] * last), own, other, choice)


def transfer_kernel(nodes, info, own, other, *refs):
    basis, out = refs[:nodes], refs[nodes]
    for m in range(nodes):
        place = 0 if nodes == 1 else (info[2] if m == 1 else 1 - info[2])
        put_transfer(out, place, info[3], own[m], other[m], basis[m][0])


def transfer(info, own, other, basis):
    nodes = len(basis)
    return pl.pallas_call(
        functools.partial(transfer_kernel, nodes),
        out_shape=jax.ShapeDtypeStruct((1, nodes, 256, 128), F32),
        in_specs=[SMEM] + [VMEM] * (2 + nodes),
        out_specs=VMEM,
        compiler_params=pltpu.CompilerParams(vmem_limit_bytes=24 << 20),
        cost_estimate=pl.CostEstimate(
            flops=nodes * 50_000_000, bytes_accessed=nodes * 600_000, transcendentals=0
        ),
    )(info, own, other, *basis)


def shifted(value, axis, by):
    count = lax.axis_size(axis)
    return lax.ppermute(value, axis, [(i, (i + by) % count) for i in range(count)])


def swapped(value, apart):
    count = lax.axis_size("leaf")
    return lax.ppermute(value, "leaf", [(i, i ^ apart) for i in range(count)])


def one_hot(skeleton, group, members, side):
    chosen = lax.dynamic_slice_in_dim(skeleton, group, 1, axis=1)[:, 0]
    chosen = jnp.concatenate(
        [lax.dynamic_slice_in_dim(chosen, k, 1, axis=0) for k in members], axis=0
    )
    target = chosen + 128 * side - 256 * side * (chosen >= 128)
    return (target[:, :, None] == lax.broadcasted_iota(jnp.int32, (1, 1, 256), 2)).astype(BF)


def local(samples, near_tiles, columns, tile_count, skeleton_one, skeleton_two, skeleton_three):
    d = lax.axis_index("leaf")
    x = lax.axis_index("cols")
    b0, b1, b2 = d & 1, (d >> 1) & 1, (d >> 2) & 1
    infos = [
        jnp.stack([x, b0, b1, side]).astype(jnp.int32) for side in (b0, b1, b2)
    ]

    near_columns = jnp.clip(columns - (d - 1) * 16, 0, 47).astype(BF).T
    block = jnp.concatenate([samples, jnp.pad(near_columns, ((0, 12), (0, 240)))], axis=0)
    by_one, by_three, by_two = (shifted(block, "cols", by) for by in (1, 3, 2))
    one, two, three = (
        lax.dynamic_slice_in_dim(near_tiles, (x + by) % 4 * 4, 4, axis=0) for by in (1, 2, 3)
    )
    tiles_one = shifted(one, "cols", 1)
    tiles_three = shifted(three, "cols", 3)
    two, tiles_one, tiles_three = lax.optimization_barrier((two, tiles_one, tiles_three))
    received = [tiles_one, shifted(two, "cols", 2), tiles_three]
    own, cols = gathered([block, by_one, by_two, by_three])
    leaves = lax.axis_size("leaf")
    rising = [(i, i + 1) for i in range(leaves - 1)]
    before = lax.ppermute(own, "leaf", rising)
    after = lax.ppermute(own, "leaf", [(j, i) for i, j in rising])

    choice_one = one_hot(skeleton_one, d >> 1, (b0 + 2 - 2 * b1, b0 + 2 * b1), b0)
    choice_two = one_hot(skeleton_two, d >> 2, (d & 3,), b1)
    choice_three = one_hot(skeleton_three, d >> 3, (d & 3,), b2)

    send, keep = near(
        infos[0], cols, tile_count, near_tiles, received, before, own, after
    )
    other = swapped(send, 1)
    away, basis = merge(keep, other, choice_one)
    arrived = swapped(away, 2)
    out_one = transfer(infos[0], keep, other, (away, basis))
    (basis_two,) = merge(basis, arrived, choice_two)
    arrived_two = swapped(basis_two, 4)
    out_two = transfer(infos[1], basis, arrived, (basis_two,))
    top, out_three = merge(basis_two, arrived_two, choice_three, infos[2])
    return out_one, out_two, out_three, top[None]


def solution(mesh):
    placed = (
        P(("leaf", "cols"), None),
        P("leaf", "cols", None, None),
        P("leaf", "cols"),
        P("leaf"),
        P("cols", None, None),
        P("cols", None, None),
        P("cols", None, None),
    )
    return jax.shard_map(
        local,
        mesh=mesh,
        in_specs=placed,
        out_specs=(P("leaf", "cols", None, None),) * 4,
        check_vma=False,
    )
```

```python
import functools

import jax
import jax.numpy as jnp
from jax import lax
from jax.experimental import pallas as pl
from jax.experimental.pallas import tpu as pltpu
from jax.sharding import PartitionSpec as P

RIDGE = 0.25
BF = jnp.bfloat16
F32 = jnp.float32
PANEL = 16


def dot(a, b, ca, cb):
    return lax.dot_general(a, b, (((ca,), (cb,)), ((), ())), preferred_element_type=F32)


def split2(x):
    hi = x.astype(BF)
    lo = (x - hi.astype(F32)).astype(BF)
    return hi, lo


def split3(x):
    hi = x.astype(BF)
    rest = x - hi.astype(F32)
    mid = rest.astype(BF)
    lo = (rest - mid.astype(F32)).astype(BF)
    return hi, mid, lo


ANY = pl.BlockSpec(memory_space=pl.ANY)
VMEM = pl.BlockSpec(memory_space=pltpu.VMEM)
SMEM = pl.BlockSpec(memory_space=pltpu.SMEM)
ROOM = pltpu.CompilerParams(vmem_limit_bytes=16 << 20)


def near_kernel(
    info, cols, counts, own_tiles, tiles_a, tiles_b, tiles_c, _, before, own, after,
    send_ref, keep_ref, win, tiles, sem,
):
    x = info[0]
    even = info[1]
    late = info[2]
    windows = [
        pltpu.make_async_copy(own, win.at[pl.ds(2048, 2048)], sem.at[0]),
        pltpu.make_async_copy(before, win.at[pl.ds(0, 2048)], sem.at[1]),
        pltpu.make_async_copy(after, win.at[pl.ds(4096, 2048)], sem.at[2]),
    ]
    arrivals = [pltpu.make_async_copy(own_tiles.at[pl.ds(x * 4, 4)], tiles.at[0], sem.at[3])]
    arrivals += [
        pltpu.make_async_copy(part, tiles.at[i + 1], sem.at[i + 4])
        for i, part in enumerate((tiles_a, tiles_b, tiles_c))
    ]
    for copy in windows + arrivals:
        copy.start()
    for copy in windows:
        copy.wait()
    for q in range(4):
        keep, slot = divmod(q, 2)
        parity = even if keep == 1 else 1 - even
        k = parity + 2 * (late if slot == 1 else 1 - late)
        count = counts[x * 4 + k]
        total = jnp.zeros((128, 256), F32)
        for delta in range(4):
            if q == 0:
                arrivals[delta].wait()
            source = (x + 4 - delta) % 4
            for s in range(0, 4, 2):
                pieces = []
                rows = []
                for t in (s, s + 1):
                    place = source * 4 + t
                    live = jnp.where(place < count, 1.0, 0.0).astype(F32)
                    piece = tiles[delta, k, t]
                    pieces.append(piece * jnp.full((128, 128), live, F32).astype(BF))
                    col = jnp.clip(cols[delta * 4 + t, x * 4 + k], 0, 47)
                    member = col & 15
                    col = (col - member) + ((x - (member >> 2)) & 3) * 4 + (member & 3)
                    rows.append(win[pl.ds(pl.multiple_of(col * 128, 128), 128), :])
                total = total + dot(
                    jnp.concatenate(pieces, axis=1), jnp.concatenate(rows, axis=0), 1, 0
                )
        if keep == 1:
            keep_ref[slot] = total
        else:
            send_ref[slot] = total


def near(info, cols, counts, own_tiles, received, before, own, after):
    block = jax.ShapeDtypeStruct((2, 128, 256), F32)
    return pl.pallas_call(
        near_kernel,
        out_shape=(block, block),
        in_specs=[SMEM] * 3 + [ANY] * 8,
        out_specs=(VMEM, VMEM),
        scratch_shapes=[
            pltpu.VMEM((6144, 256), BF),
            pltpu.VMEM((4, 4, 4, 128, 128), BF),
            pltpu.SemaphoreType.DMA((7,)),
        ],
        compiler_params=ROOM,
        cost_estimate=pl.CostEstimate(
            flops=540_000_000, bytes_accessed=6_000_000, transcendentals=0
        ),
    )(info, cols, counts, own_tiles, *received, before, own, after)


def eliminate(j, gram, rhs):
    base = j * PANEL
    half = PANEL // 2
    rows = lax.broadcasted_iota(jnp.int32, (half, 128), 0)
    a = [gram[base + half * h : base + half * (h + 1), :] for h in range(2)]
    body = [
        [a[h]] + [rhs[base + half * h : base + half * (h + 1), 128 * c : 128 * (c + 1)] for c in range(2)]
        for h in range(2)
    ]
    column = [
        [jnp.broadcast_to(a[h][:, base + k : base + k + 1], (half, 128)) for k in range(PANEL)]
        for h in range(2)
    ]
    scale = [jnp.zeros((half, 128), F32) for _ in range(2)]
    for i in range(PANEL):
        h0, r = divmod(i, half)
        pivot = column[h0][i][r : r + 1, :]
        inverse = lax.rsqrt(pivot)
        reciprocal = inverse * inverse
        scale[h0] = jnp.where(rows == r, jnp.broadcast_to(inverse, (half, 128)), scale[h0])
        factor = {}
        for h in range(h0, 2):
            value = column[h][i] * reciprocal
            factor[h] = jnp.where(rows > r, value, 0.0) if h == h0 else value
        for k in range(i + 1, PANEL):
            row = column[h0][k][r : r + 1, :]
            for h in range(h0, 2):
                column[h][k] = column[h][k] - factor[h] * row
        for c in range(3):
            row = body[h0][c][r : r + 1, :]
            for h in range(h0, 2):
                body[h][c] = body[h][c] - factor[h] * row
    return jnp.concatenate(
        [jnp.concatenate([body[h][c] * scale[h] for c in range(3)], axis=1) for h in range(2)],
        axis=0,
    )


def put_transfer(out, place, side, own, other, basis):
    zh, zl = split2(basis)
    right = jnp.concatenate([zh, zl, zh], axis=1)
    for part, at in ((own, side), (other, 1 - side)):
        ch, cl = split2(part)
        value = dot(jnp.concatenate([ch, ch, cl], axis=1), right, 1, 1) * (1.0 / 256)
        out[0, place, pl.ds(pl.multiple_of(at * 128, 128), 128), :] = value


def merge_kernel(nodes, last, *refs):
    info = None
    if last:
        info, refs = refs[0], refs[1:]
    own, other, choice = refs[:3]
    outs, gram = refs[3 : 3 + nodes], refs[-1]
    for m in range(nodes):
        wide = [jnp.concatenate(pair, axis=0) for pair in zip(split3(own[m]), split3(other[m]))]
        hi, mid, lo = (dot(choice[m], part, 1, 0) for part in wide)
        outs[m][0] = hi + (mid + lo)
        hi = hi.astype(BF)
        mid = mid.astype(BF)
        product = dot(
            jnp.concatenate([hi, hi, mid], axis=1), jnp.concatenate([hi, mid, hi], axis=1), 1, 1
        )
        on = lax.broadcasted_iota(jnp.int32, (128, 128), 0) == lax.broadcasted_iota(
            jnp.int32, (128, 128), 1
        )
        gram[m] = product * (1.0 / 256) + jnp.where(on, RIDGE, 0.0)
    for j in range(128 // PANEL):
        done = (j + 1) * PANEL
        for m in range(nodes):
            rows = eliminate(j, gram.at[m], outs[m].at[0])
            outs[m][0, j * PANEL : done, :] = rows[:, 128:]
            if done < 128:
                hi, mid, lo = split3(rows)
                left = jnp.concatenate([hi, hi, mid, mid, hi, lo], axis=0)[:, :128]
                right = jnp.concatenate([hi, mid, hi, mid, lo, hi], axis=0)
                update = dot(left, right, 0, 0)
                gram[m, done:, :] = gram[m, done:, :] - update[done:, :128]
                outs[m][0, done:, :] = outs[m][0, done:, :] - update[done:, 128:]
    if last:
        put_transfer(refs[3 + nodes], 0, info[3], own[0], other[0], outs[0][0])


def merge(own, other, choice, info=None):
    nodes = own.shape[0]
    last = info is not None
    shapes = [jax.ShapeDtypeStruct((1, 128, 256), F32)] * nodes
    if last:
        shapes.append(jax.ShapeDtypeStruct((1, 1, 256, 128), F32))
    return pl.pallas_call(
        functools.partial(merge_kernel, nodes, last),
        out_shape=tuple(shapes),
        in_specs=[SMEM] * last + [VMEM] * 3,
        out_specs=(VMEM,) * len(shapes),
        scratch_shapes=[pltpu.VMEM((nodes, 128, 128), F32)],
        compiler_params=ROOM,
        cost_estimate=pl.CostEstimate(
            flops=nodes * 40_000_000, bytes_accessed=nodes * 600_000, transcendentals=0
        ),
    )(*([info] * last), own, other, choice)


def transfer_kernel(nodes, info, own, other, *refs):
    basis, out = refs[:nodes], refs[nodes]
    for m in range(nodes):
        place = 0 if nodes == 1 else (info[2] if m == 1 else 1 - info[2])
        put_transfer(out, place, info[3], own[m], other[m], basis[m][0])


def transfer(info, own, other, basis):
    nodes = len(basis)
    return pl.pallas_call(
        functools.partial(transfer_kernel, nodes),
        out_shape=jax.ShapeDtypeStruct((1, nodes, 256, 128), F32),
        in_specs=[SMEM] + [VMEM] * (2 + nodes),
        out_specs=VMEM,
        compiler_params=pltpu.CompilerParams(vmem_limit_bytes=24 << 20),
        cost_estimate=pl.CostEstimate(
            flops=nodes * 50_000_000, bytes_accessed=nodes * 600_000, transcendentals=0
        ),
    )(info, own, other, *basis)


def shifted(value, axis, by):
    count = lax.axis_size(axis)
    return lax.ppermute(value, axis, [(i, (i + by) % count) for i in range(count)])


def swapped(value, apart):
    count = lax.axis_size("leaf")
    return lax.ppermute(value, "leaf", [(i, i ^ apart) for i in range(count)])


def one_hot(skeleton, group, members, side):
    chosen = lax.dynamic_slice_in_dim(skeleton, group, 1, axis=1)[:, 0]
    chosen = jnp.concatenate(
        [lax.dynamic_slice_in_dim(chosen, k, 1, axis=0) for k in members], axis=0
    )
    target = chosen + 128 * side - 256 * side * (chosen >= 128)
    return (target[:, :, None] == lax.broadcasted_iota(jnp.int32, (1, 1, 256), 2)).astype(BF)


def local(samples, near_tiles, columns, tile_count, skeleton_one, skeleton_two, skeleton_three):
    d = lax.axis_index("leaf")
    x = lax.axis_index("cols")
    b0, b1, b2 = d & 1, (d >> 1) & 1, (d >> 2) & 1
    infos = [
        jnp.stack([x, b0, b1, side]).astype(jnp.int32) for side in (b0, b1, b2)
    ]

    near_columns = jnp.clip(columns - (d - 1) * 16, 0, 47).astype(BF).T
    block = jnp.concatenate([samples, jnp.pad(near_columns, ((0, 12), (0, 240)))], axis=0)
    by_one, by_three, by_two = (shifted(block, "cols", by) for by in (1, 3, 2))
    one, two, three = (
        lax.dynamic_slice_in_dim(near_tiles, (x + by) % 4 * 4, 4, axis=0) for by in (1, 2, 3)
    )
    tiles_one = shifted(one, "cols", 1)
    tiles_three = shifted(three, "cols", 3)
    tiles_one, tiles_three = lax.optimization_barrier((tiles_one, tiles_three))
    tie = swapped(tiles_one, 1)
    own = jnp.concatenate([samples] + [part[:512] for part in (by_one, by_two, by_three)], axis=0)
    cols = jnp.concatenate([part[512:516, :16] for part in (block, by_one, by_two, by_three)])
    own, two, cols = lax.optimization_barrier((own, two, cols.astype(jnp.int32)))
    received = [tiles_one, shifted(two, "cols", 2), tiles_three, tie]
    leaves = lax.axis_size("leaf")
    rising = [(i, i + 1) for i in range(leaves - 1)]
    before = lax.ppermute(own, "leaf", rising)
    after = lax.ppermute(own, "leaf", [(j, i) for i, j in rising])

    choice_one = one_hot(skeleton_one, d >> 1, (b0 + 2 - 2 * b1, b0 + 2 * b1), b0)
    choice_two = one_hot(skeleton_two, d >> 2, (d & 3,), b1)
    choice_three = one_hot(skeleton_three, d >> 3, (d & 3,), b2)

    send, keep = near(
        infos[0], cols, tile_count, near_tiles, received, before, own, after
    )
    other = swapped(send, 1)
    away, basis = merge(keep, other, choice_one)
    arrived = swapped(away, 2)
    out_one = transfer(infos[0], keep, other, (away, basis))
    (basis_two,) = merge(basis, arrived, choice_two)
    arrived_two = swapped(basis_two, 4)
    out_two = transfer(infos[1], basis, arrived, (basis_two,))
    top, out_three = merge(basis_two, arrived_two, choice_three, infos[2])
    return out_one, out_two, out_three, top[None]


def solution(mesh):
    placed = (
        P(("leaf", "cols"), None),
        P("leaf", "cols", None, None),
        P("leaf", "cols"),
        P("leaf"),
        P("cols", None, None),
        P("cols", None, None),
        P("cols", None, None),
    )
    return jax.shard_map(
        local,
        mesh=mesh,
        in_specs=placed,
        out_specs=(P("leaf", "cols", None, None),) * 4,
        check_vma=False,
    )
```

```python
import functools

import jax
import jax.numpy as jnp
from jax import lax
from jax.experimental import pallas as pl
from jax.experimental.pallas import tpu as pltpu
from jax.sharding import PartitionSpec as P

RIDGE = 0.25
BF = jnp.bfloat16
F32 = jnp.float32
PANEL = 32


def dot(a, b, ca, cb):
    return lax.dot_general(a, b, (((ca,), (cb,)), ((), ())), preferred_element_type=F32)


def split2(x):
    hi = x.astype(BF)
    lo = (x - hi.astype(F32)).astype(BF)
    return hi, lo


def split3(x):
    hi = x.astype(BF)
    rest = x - hi.astype(F32)
    mid = rest.astype(BF)
    lo = (rest - mid.astype(F32)).astype(BF)
    return hi, mid, lo


ANY = pl.BlockSpec(memory_space=pl.ANY)
VMEM = pl.BlockSpec(memory_space=pltpu.VMEM)
SMEM = pl.BlockSpec(memory_space=pltpu.SMEM)
ROOM = pltpu.CompilerParams(vmem_limit_bytes=16 << 20)


def near_kernel(
    info, cols, counts, own_tiles, tiles_a, tiles_b, tiles_c, _, before, own, after,
    send_ref, keep_ref, win, tiles, sem,
):
    x = info[0]
    even = info[1]
    late = info[2]
    windows = [
        pltpu.make_async_copy(own, win.at[pl.ds(2048, 2048)], sem.at[0]),
        pltpu.make_async_copy(before, win.at[pl.ds(0, 2048)], sem.at[1]),
        pltpu.make_async_copy(after, win.at[pl.ds(4096, 2048)], sem.at[2]),
    ]
    arrivals = [pltpu.make_async_copy(own_tiles.at[pl.ds(x * 4, 4)], tiles.at[0], sem.at[3])]
    arrivals += [
        pltpu.make_async_copy(part, tiles.at[i + 1], sem.at[i + 4])
        for i, part in enumerate((tiles_a, tiles_b, tiles_c))
    ]
    for copy in windows + arrivals:
        copy.start()
    for copy in windows:
        copy.wait()
    for q in range(4):
        keep, slot = divmod(q, 2)
        parity = even if keep == 1 else 1 - even
        k = parity + 2 * (late if slot == 1 else 1 - late)
        count = counts[x * 4 + k]
        total = jnp.zeros((128, 256), F32)
        for delta in range(4):
            if q == 0:
                arrivals[delta].wait()
            source = (x + 4 - delta) % 4
            for s in range(0, 4, 2):
                pieces = []
                rows = []
                for t in (s, s + 1):
                    place = source * 4 + t
                    live = jnp.where(place < count, 1.0, 0.0).astype(F32)
                    piece = tiles[delta, k, t]
                    pieces.append(piece * jnp.full((128, 128), live, F32).astype(BF))
                    col = jnp.clip(cols[delta * 4 + t, x * 4 + k], 0, 47)
                    member = col & 15
                    col = (col - member) + ((x - (member >> 2)) & 3) * 4 + (member & 3)
                    rows.append(win[pl.ds(pl.multiple_of(col * 128, 128), 128), :])
                total = total + dot(
                    jnp.concatenate(pieces, axis=1), jnp.concatenate(rows, axis=0), 1, 0
                )
        if keep == 1:
            keep_ref[slot] = total
        else:
            send_ref[slot] = total


def near(info, cols, counts, own_tiles, received, before, own, after):
    block = jax.ShapeDtypeStruct((2, 128, 256), F32)
    return pl.pallas_call(
        near_kernel,
        out_shape=(block, block),
        in_specs=[SMEM] * 3 + [ANY] * 8,
        out_specs=(VMEM, VMEM),
        scratch_shapes=[
            pltpu.VMEM((6144, 256), BF),
            pltpu.VMEM((4, 4, 4, 128, 128), BF),
            pltpu.SemaphoreType.DMA((7,)),
        ],
        compiler_params=ROOM,
        cost_estimate=pl.CostEstimate(
            flops=540_000_000, bytes_accessed=6_000_000, transcendentals=0
        ),
    )(info, cols, counts, own_tiles, *received, before, own, after)


def sweep(body, lane, first, rows):
    column = {
        h: [jnp.broadcast_to(body[h][0][:, lane + k : lane + k + 1], (8, 128)) for k in range(16)]
        for h in range(first, len(body))
    }
    scale = [jnp.zeros((8, 128), F32) for _ in range(2)]
    for i in range(16):
        low, r = divmod(i, 8)
        h0 = first + low
        inverse = lax.rsqrt(column[h0][i][r : r + 1, :])
        reciprocal = inverse * inverse
        scale[low] = jnp.where(rows == r, jnp.broadcast_to(inverse, (8, 128)), scale[low])
        factor = {}
        for h in range(h0, len(body)):
            value = column[h][i] * reciprocal
            factor[h] = jnp.where(rows > r, value, 0.0) if h == h0 else value
        for k in range(i + 1, 16):
            row = column[h0][k][r : r + 1, :]
            for h in range(h0, len(body)):
                column[h][k] = column[h][k] - factor[h] * row
        for c in range(3):
            row = body[h0][c][r : r + 1, :]
            for h in range(h0, len(body)):
                body[h][c] = body[h][c] - factor[h] * row
    return scale


def eliminate(j, gram, rhs):
    base = j * PANEL
    halves = PANEL // 8
    rows = lax.broadcasted_iota(jnp.int32, (8, 128), 0)
    body = [
        [gram[base + 8 * h : base + 8 * (h + 1), :]]
        + [rhs[base + 8 * h : base + 8 * (h + 1), 128 * c : 128 * (c + 1)] for c in range(2)]
        for h in range(halves)
    ]
    scale = []
    for first in range(0, halves, 2):
        scale += sweep(body, base + 8 * first, first, rows)
    return jnp.concatenate(
        [jnp.concatenate([part * scale[h] for part in body[h]], axis=1) for h in range(halves)],
        axis=0,
    )


def put_transfer(out, place, side, own, other, basis):
    zh, zl = split2(basis)
    right = jnp.concatenate([zh, zl, zh], axis=1)
    for part, at in ((own, side), (other, 1 - side)):
        ch, cl = split2(part)
        value = dot(jnp.concatenate([ch, ch, cl], axis=1), right, 1, 1) * (1.0 / 256)
        out[0, place, pl.ds(pl.multiple_of(at * 128, 128), 128), :] = value


def merge_kernel(nodes, last, *refs):
    info = None
    if last:
        info, refs = refs[0], refs[1:]
    own, other, choice = refs[:3]
    outs, gram = refs[3 : 3 + nodes], refs[-1]
    for m in range(nodes):
        wide = [jnp.concatenate(pair, axis=0) for pair in zip(split3(own[m]), split3(other[m]))]
        hi, mid, lo = (dot(choice[m], part, 1, 0) for part in wide)
        outs[m][0] = hi + (mid + lo)
        hi = hi.astype(BF)
        mid = mid.astype(BF)
        product = dot(
            jnp.concatenate([hi, hi, mid], axis=1), jnp.concatenate([hi, mid, hi], axis=1), 1, 1
        )
        on = lax.broadcasted_iota(jnp.int32, (128, 128), 0) == lax.broadcasted_iota(
            jnp.int32, (128, 128), 1
        )
        gram[m] = product * (1.0 / 256) + jnp.where(on, RIDGE, 0.0)
    for j in range(128 // PANEL):
        done = (j + 1) * PANEL
        for m in range(nodes):
            rows = eliminate(j, gram.at[m], outs[m].at[0])
            outs[m][0, j * PANEL : done, :] = rows[:, 128:]
            if done < 128:
                hi, mid = split2(rows)
                left = jnp.concatenate([hi, hi, mid, mid], axis=0)[:, :128]
                right = jnp.concatenate([hi, mid, hi, mid], axis=0)
                update = dot(left, right, 0, 0)
                gram[m, done:, :] = gram[m, done:, :] - update[done:, :128]
                outs[m][0, done:, :] = outs[m][0, done:, :] - update[done:, 128:]
    if last:
        put_transfer(refs[3 + nodes], 0, info[3], own[0], other[0], outs[0][0])


def merge(own, other, choice, info=None):
    nodes = own.shape[0]
    last = info is not None
    shapes = [jax.ShapeDtypeStruct((1, 128, 256), F32)] * nodes
    if last:
        shapes.append(jax.ShapeDtypeStruct((1, 1, 256, 128), F32))
    return pl.pallas_call(
        functools.partial(merge_kernel, nodes, last),
        out_shape=tuple(shapes),
        in_specs=[SMEM] * last + [VMEM] * 3,
        out_specs=(VMEM,) * len(shapes),
        scratch_shapes=[pltpu.VMEM((nodes, 128, 128), F32)],
        compiler_params=ROOM,
        cost_estimate=pl.CostEstimate(
            flops=nodes * 40_000_000, bytes_accessed=nodes * 600_000, transcendentals=0
        ),
    )(*([info] * last), own, other, choice)


def transfer_kernel(nodes, info, own, other, *refs):
    basis, out = refs[:nodes], refs[nodes]
    for m in range(nodes):
        place = 0 if nodes == 1 else (info[2] if m == 1 else 1 - info[2])
        put_transfer(out, place, info[3], own[m], other[m], basis[m][0])


def transfer(info, own, other, basis):
    nodes = len(basis)
    return pl.pallas_call(
        functools.partial(transfer_kernel, nodes),
        out_shape=jax.ShapeDtypeStruct((1, nodes, 256, 128), F32),
        in_specs=[SMEM] + [VMEM] * (2 + nodes),
        out_specs=VMEM,
        compiler_params=pltpu.CompilerParams(vmem_limit_bytes=24 << 20),
        cost_estimate=pl.CostEstimate(
            flops=nodes * 50_000_000, bytes_accessed=nodes * 600_000, transcendentals=0
        ),
    )(info, own, other, *basis)


def shifted(value, axis, by):
    count = lax.axis_size(axis)
    return lax.ppermute(value, axis, [(i, (i + by) % count) for i in range(count)])


def swapped(value, apart):
    count = lax.axis_size("leaf")
    return lax.ppermute(value, "leaf", [(i, i ^ apart) for i in range(count)])


def one_hot(skeleton, group, members, side):
    chosen = lax.dynamic_slice_in_dim(skeleton, group, 1, axis=1)[:, 0]
    chosen = jnp.concatenate(
        [lax.dynamic_slice_in_dim(chosen, k, 1, axis=0) for k in members], axis=0
    )
    target = chosen + 128 * side - 256 * side * (chosen >= 128)
    return (target[:, :, None] == lax.broadcasted_iota(jnp.int32, (1, 1, 256), 2)).astype(BF)


def local(samples, near_tiles, columns, tile_count, skeleton_one, skeleton_two, skeleton_three):
    d = lax.axis_index("leaf")
    x = lax.axis_index("cols")
    b0, b1, b2 = d & 1, (d >> 1) & 1, (d >> 2) & 1
    infos = [
        jnp.stack([x, b0, b1, side]).astype(jnp.int32) for side in (b0, b1, b2)
    ]

    near_columns = jnp.clip(columns - (d - 1) * 16, 0, 47).astype(BF).T
    block = jnp.concatenate([samples, jnp.pad(near_columns, ((0, 12), (0, 240)))], axis=0)
    by_one, by_three, by_two = (shifted(block, "cols", by) for by in (1, 3, 2))
    one, two, three = (
        lax.dynamic_slice_in_dim(near_tiles, (x + by) % 4 * 4, 4, axis=0) for by in (1, 2, 3)
    )
    tiles_one = shifted(one, "cols", 1)
    tiles_three = shifted(three, "cols", 3)
    tiles_one, tiles_three = lax.optimization_barrier((tiles_one, tiles_three))
    tie = swapped(tiles_one, 1)
    own = jnp.concatenate([samples] + [part[:512] for part in (by_one, by_two, by_three)], axis=0)
    cols = jnp.concatenate([part[512:516, :16] for part in (block, by_one, by_two, by_three)]).astype(jnp.int32)
    own, two = lax.optimization_barrier((own, two))
    received = [tiles_one, shifted(two, "cols", 2), tiles_three, tie]
    leaves = lax.axis_size("leaf")
    rising = [(i, i + 1) for i in range(leaves - 1)]
    before = lax.ppermute(own, "leaf", rising)
    after = lax.ppermute(own, "leaf", [(j, i) for i, j in rising])

    choice_one = one_hot(skeleton_one, d >> 1, (b0 + 2 - 2 * b1, b0 + 2 * b1), b0)
    choice_two = one_hot(skeleton_two, d >> 2, (d & 3,), b1)
    choice_three = one_hot(skeleton_three, d >> 3, (d & 3,), b2)

    send, keep = near(
        infos[0], cols, tile_count, near_tiles, received, before, own, after
    )
    other = swapped(send, 1)
    away, basis = merge(keep, other, choice_one)
    arrived = swapped(away, 2)
    out_one = transfer(infos[0], keep, other, (away, basis))
    (basis_two,) = merge(basis, arrived, choice_two)
    arrived_two = swapped(basis_two, 4)
    out_two = transfer(infos[1], basis, arrived, (basis_two,))
    top, out_three = merge(basis_two, arrived_two, choice_three, infos[2])
    return out_one, out_two, out_three, top[None]


def solution(mesh):
    placed = (
        P(("leaf", "cols"), None),
        P("leaf", "cols", None, None),
        P("leaf", "cols"),
        P("leaf"),
        P("cols", None, None),
        P("cols", None, None),
        P("cols", None, None),
    )
    return jax.shard_map(
        local,
        mesh=mesh,
        in_specs=placed,
        out_specs=(P("leaf", "cols", None, None),) * 4,
        check_vma=False,
    )
```

```python
import functools

import jax
import jax.numpy as jnp
from jax import lax
from jax.experimental import pallas as pl
from jax.experimental.pallas import tpu as pltpu
from jax.sharding import PartitionSpec as P

RIDGE = 0.25
BF = jnp.bfloat16
F32 = jnp.float32
PANEL = 32


def dot(a, b, ca, cb):
    return lax.dot_general(a, b, (((ca,), (cb,)), ((), ())), preferred_element_type=F32)


def split2(x):
    hi = x.astype(BF)
    lo = (x - hi.astype(F32)).astype(BF)
    return hi, lo


def split3(x):
    hi = x.astype(BF)
    rest = x - hi.astype(F32)
    mid = rest.astype(BF)
    lo = (rest - mid.astype(F32)).astype(BF)
    return hi, mid, lo


ANY = pl.BlockSpec(memory_space=pl.ANY)
VMEM = pl.BlockSpec(memory_space=pltpu.VMEM)
SMEM = pl.BlockSpec(memory_space=pltpu.SMEM)
ROOM = pltpu.CompilerParams(vmem_limit_bytes=16 << 20)


def near_kernel(
    info, cols, counts, own_tiles, tiles_a, tiles_b, tiles_c, _, before, own, after,
    send_ref, keep_ref, win, tiles, sem,
):
    x = info[0]
    even = info[1]
    late = info[2]
    windows = [
        pltpu.make_async_copy(own, win.at[pl.ds(2048, 2048)], sem.at[0]),
        pltpu.make_async_copy(before, win.at[pl.ds(0, 2048)], sem.at[1]),
        pltpu.make_async_copy(after, win.at[pl.ds(4096, 2048)], sem.at[2]),
    ]
    arrivals = [pltpu.make_async_copy(own_tiles.at[pl.ds(x * 4, 4)], tiles.at[0], sem.at[3])]
    arrivals += [
        pltpu.make_async_copy(part, tiles.at[i + 1], sem.at[i + 4])
        for i, part in enumerate((tiles_a, tiles_b, tiles_c))
    ]
    for copy in windows + arrivals:
        copy.start()
    for copy in windows:
        copy.wait()
    for q in range(4):
        keep, slot = divmod(q, 2)
        parity = even if keep == 1 else 1 - even
        k = parity + 2 * (late if slot == 1 else 1 - late)
        count = counts[x * 4 + k]
        total = jnp.zeros((128, 256), F32)
        for delta in range(4):
            if q == 0:
                arrivals[delta].wait()
            source = (x + 4 - delta) % 4
            for s in range(0, 4, 2):
                pieces = []
                rows = []
                for t in (s, s + 1):
                    place = source * 4 + t
                    live = jnp.where(place < count, 1.0, 0.0).astype(F32)
                    piece = tiles[delta, k, t]
                    pieces.append(piece * jnp.full((128, 128), live, F32).astype(BF))
                    col = jnp.clip(cols[delta * 4 + t, x * 4 + k], 0, 47)
                    member = col & 15
                    col = (col - member) + ((x - (member >> 2)) & 3) * 4 + (member & 3)
                    rows.append(win[pl.ds(pl.multiple_of(col * 128, 128), 128), :])
                total = total + dot(
                    jnp.concatenate(pieces, axis=1), jnp.concatenate(rows, axis=0), 1, 0
                )
        if keep == 1:
            keep_ref[slot] = total
        else:
            send_ref[slot] = total


def near(info, cols, counts, own_tiles, received, before, own, after):
    block = jax.ShapeDtypeStruct((2, 128, 256), F32)
    return pl.pallas_call(
        near_kernel,
        out_shape=(block, block),
        in_specs=[SMEM] * 3 + [ANY] * 8,
        out_specs=(VMEM, VMEM),
        scratch_shapes=[
            pltpu.VMEM((6144, 256), BF),
            pltpu.VMEM((4, 4, 4, 128, 128), BF),
            pltpu.SemaphoreType.DMA((7,)),
        ],
        compiler_params=ROOM,
        cost_estimate=pl.CostEstimate(
            flops=540_000_000, bytes_accessed=6_000_000, transcendentals=0
        ),
    )(info, cols, counts, own_tiles, *received, before, own, after)


def sweep(body, lane, first, rows):
    column = {
        h: [jnp.broadcast_to(body[h][0][:, lane + k : lane + k + 1], (8, 128)) for k in range(16)]
        for h in range(first, len(body))
    }
    scale = [jnp.zeros((8, 128), F32) for _ in range(2)]
    for i in range(16):
        low, r = divmod(i, 8)
        h0 = first + low
        inverse = lax.rsqrt(column[h0][i][r : r + 1, :])
        reciprocal = inverse * inverse
        scale[low] = jnp.where(rows == r, jnp.broadcast_to(inverse, (8, 128)), scale[low])
        factor = {}
        for h in range(h0, len(body)):
            value = column[h][i] * reciprocal
            factor[h] = jnp.where(rows > r, value, 0.0) if h == h0 else value
        for k in range(i + 1, 16):
            row = column[h0][k][r : r + 1, :]
            for h in range(h0, len(body)):
                column[h][k] = column[h][k] - factor[h] * row
        for c in range(3):
            row = body[h0][c][r : r + 1, :]
            for h in range(h0, len(body)):
                body[h][c] = body[h][c] - factor[h] * row
    return scale


def eliminate(j, gram, rhs):
    base = j * PANEL
    halves = PANEL // 8
    rows = lax.broadcasted_iota(jnp.int32, (8, 128), 0)
    body = [
        [gram[base + 8 * h : base + 8 * (h + 1), :]]
        + [rhs[base + 8 * h : base + 8 * (h + 1), 128 * c : 128 * (c + 1)] for c in range(2)]
        for h in range(halves)
    ]
    scale = []
    for first in range(0, halves, 2):
        scale += sweep(body, base + 8 * first, first, rows)
    return jnp.concatenate(
        [jnp.concatenate([part * scale[h] for part in body[h]], axis=1) for h in range(halves)],
        axis=0,
    )


def put_transfer(out, place, side, own, other, basis):
    zh, zl = split2(basis)
    right = jnp.concatenate([zh, zl, zh], axis=1)
    for part, at in ((own, side), (other, 1 - side)):
        ch, cl = split2(part)
        value = dot(jnp.concatenate([ch, ch, cl], axis=1), right, 1, 1) * (1.0 / 256)
        out[0, place, pl.ds(pl.multiple_of(at * 128, 128), 128), :] = value


def merge_kernel(nodes, last, *refs):
    info = None
    if last:
        info, refs = refs[0], refs[1:]
    own, other, choice = refs[:3]
    outs, gram = refs[3 : 3 + nodes], refs[-1]
    for m in range(nodes):
        wide = [jnp.concatenate(pair, axis=0) for pair in zip(split3(own[m]), split3(other[m]))]
        hi, mid, lo = (dot(choice[m], part, 1, 0) for part in wide)
        outs[m][0] = hi + (mid + lo)
        hi = hi.astype(BF)
        mid = mid.astype(BF)
        product = dot(
            jnp.concatenate([hi, hi, mid], axis=1), jnp.concatenate([hi, mid, hi], axis=1), 1, 1
        )
        on = lax.broadcasted_iota(jnp.int32, (128, 128), 0) == lax.broadcasted_iota(
            jnp.int32, (128, 128), 1
        )
        gram[m] = product * (1.0 / 256) + jnp.where(on, RIDGE, 0.0)
    for j in range(128 // PANEL):
        done = (j + 1) * PANEL
        for m in range(nodes):
            rows = eliminate(j, gram.at[m], outs[m].at[0])
            outs[m][0, j * PANEL : done, :] = rows[:, 128:]
            if done < 128:
                hi, mid = split2(rows)
                left = jnp.concatenate([hi, hi, mid, mid], axis=0)[:, :128]
                right = jnp.concatenate([hi, mid, hi, mid], axis=0)
                update = dot(left, right, 0, 0)
                gram[m, done:, :] = gram[m, done:, :] - update[done:, :128]
                outs[m][0, done:, :] = outs[m][0, done:, :] - update[done:, 128:]
    if last:
        put_transfer(refs[3 + nodes], 0, info[3], own[0], other[0], outs[0][0])


def merge(own, other, choice, info=None):
    nodes = own.shape[0]
    last = info is not None
    shapes = [jax.ShapeDtypeStruct((1, 128, 256), F32)] * nodes
    if last:
        shapes.append(jax.ShapeDtypeStruct((1, 1, 256, 128), F32))
    return pl.pallas_call(
        functools.partial(merge_kernel, nodes, last),
        out_shape=tuple(shapes),
        in_specs=[SMEM] * last + [VMEM] * 3,
        out_specs=(VMEM,) * len(shapes),
        scratch_shapes=[pltpu.VMEM((nodes, 128, 128), F32)],
        compiler_params=ROOM,
        cost_estimate=pl.CostEstimate(
            flops=nodes * 40_000_000, bytes_accessed=nodes * 600_000, transcendentals=0
        ),
    )(*([info] * last), own, other, choice)


def transfer_kernel(nodes, info, own, other, *refs):
    basis, out = refs[:nodes], refs[nodes]
    for m in range(nodes):
        place = 0 if nodes == 1 else (info[2] if m == 1 else 1 - info[2])
        put_transfer(out, place, info[3], own[m], other[m], basis[m][0])


def transfer(info, own, other, basis):
    nodes = len(basis)
    return pl.pallas_call(
        functools.partial(transfer_kernel, nodes),
        out_shape=jax.ShapeDtypeStruct((1, nodes, 256, 128), F32),
        in_specs=[SMEM] + [VMEM] * (2 + nodes),
        out_specs=VMEM,
        compiler_params=pltpu.CompilerParams(vmem_limit_bytes=24 << 20),
        cost_estimate=pl.CostEstimate(
            flops=nodes * 50_000_000, bytes_accessed=nodes * 600_000, transcendentals=0
        ),
    )(info, own, other, *basis)


def shifted(value, axis, by):
    count = lax.axis_size(axis)
    return lax.ppermute(value, axis, [(i, (i + by) % count) for i in range(count)])


def swapped(value, apart):
    count = lax.axis_size("leaf")
    return lax.ppermute(value, "leaf", [(i, i ^ apart) for i in range(count)])


def one_hot(skeleton, group, members, side):
    chosen = lax.dynamic_slice_in_dim(skeleton, group, 1, axis=1)[:, 0]
    chosen = jnp.concatenate(
        [lax.dynamic_slice_in_dim(chosen, k, 1, axis=0) for k in members], axis=0
    )
    target = chosen + 128 * side - 256 * side * (chosen >= 128)
    return (target[:, :, None] == lax.broadcasted_iota(jnp.int32, (1, 1, 256), 2)).astype(BF)


def local(samples, near_tiles, columns, tile_count, skeleton_one, skeleton_two, skeleton_three):
    d = lax.axis_index("leaf")
    x = lax.axis_index("cols")
    b0, b1, b2 = d & 1, (d >> 1) & 1, (d >> 2) & 1
    infos = [
        jnp.stack([x, b0, b1, side]).astype(jnp.int32) for side in (b0, b1, b2)
    ]

    near_columns = jnp.clip(columns - (d - 1) * 16, 0, 47).astype(BF).T
    block = jnp.concatenate([samples, jnp.pad(near_columns, ((0, 12), (0, 240)))], axis=0)
    by_one, by_three, by_two = (shifted(block, "cols", by) for by in (1, 3, 2))
    one, two, three = (
        lax.dynamic_slice_in_dim(near_tiles, (x + by) % 4 * 4, 4, axis=0) for by in (1, 2, 3)
    )
    tiles_three = shifted(three, "cols", 3)
    tiles_one = shifted(one, "cols", 1)
    tiles_three, tiles_one = lax.optimization_barrier((tiles_three, tiles_one))
    tie = swapped(tiles_one, 1)
    own = jnp.concatenate([samples] + [part[:512] for part in (by_one, by_two, by_three)], axis=0)
    cols = jnp.concatenate([part[512:516, :16] for part in (block, by_one, by_two, by_three)]).astype(jnp.int32)
    own, two = lax.optimization_barrier((own, two))
    received = [tiles_one, shifted(two, "cols", 2), tiles_three, tie]
    leaves = lax.axis_size("leaf")
    rising = [(i, i + 1) for i in range(leaves - 1)]
    before = lax.ppermute(own, "leaf", rising)
    after = lax.ppermute(own, "leaf", [(j, i) for i, j in rising])

    choice_one = one_hot(skeleton_one, d >> 1, (b0 + 2 - 2 * b1, b0 + 2 * b1), b0)
    choice_two = one_hot(skeleton_two, d >> 2, (d & 3,), b1)
    choice_three = one_hot(skeleton_three, d >> 3, (d & 3,), b2)

    send, keep = near(
        infos[0], cols, tile_count, near_tiles, received, before, own, after
    )
    other = swapped(send, 1)
    away, basis = merge(keep, other, choice_one)
    arrived = swapped(away, 2)
    out_one = transfer(infos[0], keep, other, (away, basis))
    (basis_two,) = merge(basis, arrived, choice_two)
    arrived_two = swapped(basis_two, 4)
    out_two = transfer(infos[1], basis, arrived, (basis_two,))
    top, out_three = merge(basis_two, arrived_two, choice_three, infos[2])
    return out_one, out_two, out_three, top[None]


def solution(mesh):
    placed = (
        P(("leaf", "cols"), None),
        P("leaf", "cols", None, None),
        P("leaf", "cols"),
        P("leaf"),
        P("cols", None, None),
        P("cols", None, None),
        P("cols", None, None),
    )
    return jax.shard_map(
        local,
        mesh=mesh,
        in_specs=placed,
        out_specs=(P("leaf", "cols", None, None),) * 4,
        check_vma=False,
    )
```
